256 devices in a mesh: dp: 8 (over z), expert: 32 (over x, y, core).
Axes of the slice: x: 4, y: 4, z: 8, core: 2. Of those that a mesh axis runs over, the one named last changes fastest.
Arguments:
- tokens: bfloat16 [65536, 2048], P(('dp', 'expert')), may hold values from -6 to 6
- chosen_expert_index: int32 [65536, 8], P(('dp', 'expert')), may hold values from 0 to 127, as said below
- routing_gate_weight: float32 [65536, 8], P(('dp', 'expert')), may hold values from 0.1 to 1
- w_gate: bfloat16 [32, 2048, 768], P('expert'), may hold values from -0.125 to 0.125
- w_up: bfloat16 [32, 2048, 768], P('expert'), may hold values from -0.125 to 0.125
- w_down: bfloat16 [32, 768, 2048], P('expert'), may hold values from -0.21875 to 0.21875
- capacity: int32 [8, 32], P('dp', 'expert'), may hold values from 128 to 768, as said below
Outputs:
- mixed: bfloat16 [65536, 2048], P(('dp', 'expert'))
The draws below stay inside these ranges and needn't reach their ends.
Inputs may be any that keep to these rules, and one draw needn't show every extreme that they name: `chosen_expert_index`: slot k of a token names an expert among 16 k to 16 k + 15, so a token's experts differ. Among the rows of one device no expert is named by more than 32 rows, and some expert in flight is named by exactly 32 rows of each device. Some group and expert have capacity 768 in every draw.
All inputs are finite; a program needn't handle non-finite values.
Results may differ from the reference program's by a relative error of at most 0.0058.
Values may be sent and summed in bfloat16 or wider, within the bound.
A program may use at most 64 MiB of HBM per device.

```python
import math
import jax
import jax.numpy as jnp
from jax import lax

D = 2048
FF = 768
TOPK = 8
BLOCK = 128
TOK_DEV = 256
SLOT = 32
CAPMAX = 768
CAP_LO = 128
TOKENS = 65536
N_DP = 8
N_EXPERT = 32


def draw_chosen_expert_index(key, part):
    blocks = TOKENS // TOK_DEV
    half_mean = TOK_DEV // 16
    lanes = blocks * TOPK
    key_shift, key_value, key_row = jax.random.split(jax.random.fold_in(key, 11), 3)
    shifts = jax.random.randint(key_shift, (lanes, 8), 0, half_mean + 1)
    shifts = shifts.at[:, 0].set(half_mean)
    counts = jnp.concatenate([half_mean + shifts, half_mean - shifts], axis=1)
    ends = jnp.cumsum(counts, axis=1)
    spots = jnp.arange(TOK_DEV, dtype=jnp.int32)
    slot_of = jnp.sum((ends[:, None, :] <= spots[None, :, None]).astype(jnp.int32), axis=2)
    value_scores = jax.random.randint(key_value, (lanes, 16), 0, 1 << 20) * 16 + jnp.arange(16, dtype=jnp.int32)[None, :]
    value_order = jnp.argsort(value_scores, axis=1).astype(jnp.int32)
    values = jnp.take_along_axis(value_order, slot_of, axis=1)
    row_scores = jax.random.randint(key_row, (lanes, TOK_DEV), 0, 1 << 16) * TOK_DEV + spots[None, :]
    shuffle = jnp.argsort(row_scores, axis=1).astype(jnp.int32)
    values = jnp.take_along_axis(values, shuffle, axis=1)
    values = values.reshape(blocks, TOPK, TOK_DEV).transpose(0, 2, 1)
    ranges = 16 * jnp.arange(TOPK, dtype=jnp.int32)
    return (values + ranges[None, None, :]).reshape(TOKENS, TOPK).astype(jnp.int32)


def draw_capacity(key, part):
    key_value, key_spot = jax.random.split(jax.random.fold_in(key, 23))
    values = jax.random.randint(key_value, (N_DP * N_EXPERT,), CAP_LO, CAPMAX + 1)
    spot = jax.random.randint(key_spot, (), 0, N_DP * N_EXPERT)
    values = values.at[spot].set(CAPMAX)
    return values.reshape(N_DP, N_EXPERT).astype(jnp.int32)


def level_of(rng, dims, shards, least, top_value):
    def one(axis_at, shards_of):
        heights = jax.random.uniform(jax.random.fold_in(jax.random.fold_in(rng, 6), axis_at), (shards_of,), jnp.float32, least / len(shards), top_value / len(shards))
        return jnp.repeat(jnp.exp(heights), dims[axis_at] // shards_of).reshape((-1,) + (1,) * (len(dims) - axis_at - 1))

    gain = one(*shards[0])
    for cut in shards[1:]:
        gain = gain * one(*cut)
    return gain


def scatter_about(stream_key, extent, width, bound, cuts=(), kind=jnp.bfloat16):
    loudness = level_of(stream_key, extent, cuts, -0.22, 0.18) if cuts else 1.0
    result = jax.random.normal(stream_key, extent, jnp.float32) * width * loudness
    return jnp.minimum(jnp.maximum(result, -bound), bound).astype(kind)


def setup_inputs(seed: int = 0) -> dict:
    splits = jax.random.split(jax.random.key(seed), 8)
    tokens = scatter_about(splits[0], (TOKENS, D), 1.0, 6.0, ((0, 256),))
    chosen_expert_index = draw_chosen_expert_index(jax.random.fold_in(splits[7], 71), 0)
    routing_gate_weight = jnp.clip(jnp.exp(math.log(1.0) - 2.3025851 * jax.random.uniform(splits[2], (TOKENS, TOPK), jnp.float32) ** level_of(splits[2], (TOKENS, TOPK), ((0, 256),), -0.2, 0.2)), 0.1, 1.0)
    w_gate = scatter_about(splits[3], (N_EXPERT, D, FF), D ** -0.5, 0.125, ((0, 32),))
    w_up = scatter_about(splits[4], (N_EXPERT, D, FF), D ** -0.5, 0.125, ((0, 32),))
    w_down = scatter_about(splits[5], (N_EXPERT, FF, D), FF ** -0.5, 0.21875, ((0, 32),))
    capacity = draw_capacity(jax.random.fold_in(splits[7], 71), 0)
    return {"tokens": tokens, "chosen_expert_index": chosen_expert_index, "routing_gate_weight": routing_gate_weight, "w_gate": w_gate, "w_up": w_up, "w_down": w_down, "capacity": capacity}


def expert_ffn(rows, gate_matrix, up_matrix, down_matrix):
    gated = jnp.dot(rows, gate_matrix, preferred_element_type=jnp.float32)
    upward = jnp.dot(rows, up_matrix, preferred_element_type=jnp.float32)
    hidden = (jax.nn.silu(gated) * upward).astype(jnp.bfloat16)
    return jnp.dot(hidden, down_matrix, preferred_element_type=jnp.float32).astype(jnp.bfloat16)


def reference(tokens, chosen_expert_index, routing_gate_weight, w_gate, w_up, w_down, capacity):
    group_tokens = TOKENS // N_DP
    room = N_DP * min(CAPMAX + BLOCK, N_EXPERT * SLOT)
    partners = jnp.bitwise_xor(jnp.arange(N_DP, dtype=jnp.int32), jnp.int32(N_DP // 2))
    token_ids = jnp.arange(TOKENS, dtype=jnp.int32)

    def one_expert(total, inputs):
        number, gate_matrix, up_matrix, down_matrix = inputs
        matches = chosen_expert_index == number
        chosen = jnp.any(matches, axis=1)
        weight = jnp.sum(jnp.where(matches, routing_gate_weight, jnp.float32(0.0)), axis=1)
        per_group = chosen.reshape(N_DP, group_tokens).astype(jnp.int32)
        ranks = jnp.cumsum(per_group, axis=1) - 1
        load = jnp.sum(per_group, axis=1)
        limit = jnp.take(capacity, number, axis=1)
        spare = jnp.maximum(limit - load, 0)
        partner_spare = jnp.take(spare, partners)
        over = ranks - limit[:, None]
        keep = (per_group > 0) & ((ranks < limit[:, None]) | ((over >= 0) & (over < jnp.minimum(BLOCK, partner_spare)[:, None])))
        keep = keep.reshape(TOKENS)
        compact = (jnp.cumsum(keep.astype(jnp.int32)) - 1).astype(jnp.int32)
        target = jnp.where(keep, compact, jnp.int32(room)).astype(jnp.int32)
        table = jnp.zeros((room,), jnp.int32).at[target].set(token_ids, mode="drop")
        rows = jnp.take(tokens, table, axis=0)
        outputs = expert_ffn(rows, gate_matrix, up_matrix, down_matrix)
        back = jnp.take(outputs, jnp.clip(compact, 0, room - 1), axis=0).astype(jnp.float32)
        total = total + jnp.where(keep, weight, jnp.float32(0.0))[:, None] * back
        return total, None

    start = jnp.zeros((TOKENS, D), jnp.float32)
    numbers = jnp.arange(N_EXPERT, dtype=jnp.int32)
    total, _ = lax.scan(one_expert, start, (numbers, w_gate, w_up, w_down))
    return total.astype(jnp.bfloat16)
```

```python
import jax
import jax.numpy as jnp
from jax import lax
from jax.sharding import PartitionSpec as P

BLOCK = 128
SLOT = 32


def on_device(tokens, chosen_expert_index, routing_gate_weight, w_gate, w_up, w_down, capacity):
    experts = lax.axis_size("expert")
    groups = lax.axis_size("dp")
    width = tokens.shape[1]
    slots = experts // 16
    targets = jnp.arange(experts, dtype=jnp.int32)
    matches = chosen_expert_index[:, :slots, None] == targets[None, None, :]
    chosen = jnp.any(matches, axis=1)
    weight = jnp.sum(jnp.where(matches, routing_gate_weight[:, :slots, None], 0.0), axis=1)
    chosen_int = chosen.astype(jnp.int32)
    position = jnp.cumsum(chosen_int, axis=0) - 1
    counts = jnp.sum(chosen_int, axis=0)
    slot_ids = jnp.arange(SLOT, dtype=jnp.int32)
    placer = (position.T[:, None, :] == slot_ids[None, :, None]) & chosen.T[:, None, :]
    send_rows = jnp.einsum(
        "jpt,td->jpd", placer.astype(jnp.bfloat16), tokens, preferred_element_type=jnp.float32
    ).astype(jnp.bfloat16)
    arrived = lax.all_to_all(send_rows, "expert", split_axis=0, concat_axis=0, tiled=True)
    arrived_counts = lax.all_to_all(
        counts[:, None], "expert", split_axis=0, concat_axis=0, tiled=True
    )[:, 0]
    offsets = jnp.cumsum(arrived_counts) - arrived_counts
    limit = capacity[0, 0]
    spare = jnp.maximum(limit - jnp.sum(arrived_counts), 0)
    pairs = [(source, source ^ (groups // 2)) for source in range(groups)]
    partner_spare = lax.ppermute(spare[None], "dp", pairs)[0]
    total_limit = limit + jnp.minimum(BLOCK, partner_spare)
    kept = jnp.clip(total_limit - offsets, 0, arrived_counts)
    keep = (slot_ids[None, :] < kept[:, None]).reshape(-1)
    rows = arrived.reshape(experts * SLOT, width)
    gated = jnp.dot(rows, w_gate[0], preferred_element_type=jnp.float32)
    upward = jnp.dot(rows, w_up[0], preferred_element_type=jnp.float32)
    hidden = (jax.nn.silu(gated) * upward).astype(jnp.bfloat16)
    computed = jnp.dot(hidden, w_down[0], preferred_element_type=jnp.float32)
    answers = jnp.where(keep[:, None], computed, 0.0).astype(jnp.bfloat16)
    back = lax.all_to_all(
        answers.reshape(experts, SLOT, width), "expert", split_axis=0, concat_axis=0, tiled=True
    ).reshape(experts * SLOT, width)
    spread = (position[:, :, None] == slot_ids[None, None, :]) & chosen[:, :, None]
    combine = jnp.where(spread, weight[:, :, None], 0.0).reshape(-1, experts * SLOT)
    high = combine.astype(jnp.bfloat16)
    low = (combine - high.astype(jnp.float32)).astype(jnp.bfloat16)
    mixed = jnp.dot(high, back, preferred_element_type=jnp.float32) + jnp.dot(
        low, back, preferred_element_type=jnp.float32
    )
    return mixed.astype(jnp.bfloat16)


def solution(mesh):
    return jax.shard_map(
        on_device,
        mesh=mesh,
        in_specs=(
            P(("dp", "expert"), None),
            P(("dp", "expert"), None),
            P(("dp", "expert"), None),
            P("expert", None, None),
            P("expert", None, None),
            P("expert", None, None),
            P("dp", "expert"),
        ),
        out_specs=P(("dp", "expert"), None),
        check_vma=False,
    )
```

```python
import functools
import jax
import jax.numpy as jnp
from jax import lax
from jax.experimental import pallas as pl
from jax.experimental.pallas import tpu as pltpu
from jax.sharding import PartitionSpec as P

BLOCK = 128
SLOT = 32
EXPERTS = 32
PART = 8
ROWS = PART * SLOT
PARTS = EXPERTS // PART
MESH = pl.DeviceIdType.MESH
F32 = jnp.float32
BF16 = jnp.bfloat16


def step_of(r):
    dx = (r % PART) // 2
    return dx, (r // PART + dx) % 4, r % 2


def target(me, r):
    dx, dy, dc = step_of(r)
    x, y, c = me // 8, (me // 2) % 4, me % 2
    return ((x + dx) % 4) * 8 + ((y + dy) % 4) * 2 + (c + dc) % 2


def origin(me, r):
    dx, dy, dc = step_of(r)
    x, y, c = me // 8, (me // 2) % 4, me % 2
    return ((x + 4 - dx) % 4) * 8 + ((y + 4 - dy) % 4) * 2 + (c + dc) % 2


def iota(shape, axis):
    return lax.broadcasted_iota(jnp.int32, shape, axis)


def kernel(
    tokens_hbm, index_ref, gate_ref, w_gate_hbm, w_up_hbm, w_down_hbm, capacity_ref,
    mixed_ref,
    tok, w_gate, w_up, w_down, send, recv, answer, back, spot, scaled, hidden, total,
    count_out, count_in, spare_out, spare_in,
    load_sem, send_sem, recv_sem, ret_send, ret_recv, cnt_send, cnt_recv, spare_sem,
):
    me = lax.axis_index("expert")
    group = lax.axis_index("dp")
    groups = lax.axis_size("dp")
    partner = (group + groups // 2) % groups

    loads = [
        pltpu.make_async_copy(src, dst, load_sem.at[i])
        for i, (src, dst) in enumerate(
            [
                (tokens_hbm, tok),
                (w_gate_hbm.at[0], w_gate),
                (w_up_hbm.at[0], w_up),
                (w_down_hbm.at[0], w_down),
            ]
        )
    ]
    for load in loads:
        load.start()

    barrier = pltpu.get_barrier_semaphore()

    @pl.loop(1, EXPERTS)
    def _(r):
        pl.semaphore_signal(barrier, inc=1, device_id=(group, target(me, r)), device_id_type=MESH)

    pl.semaphore_signal(barrier, inc=1, device_id=(partner, me), device_id_type=MESH)

    index = index_ref[...]
    experts = iota((EXPERTS, 256), 0)
    named = (experts == index[0:1, :]) | (experts == index[1:2, :])
    named_f = named.astype(F32)
    earlier = (iota((256, 256), 0) < iota((256, 256), 1)).astype(BF16)
    place = jnp.dot(named_f.astype(BF16), earlier, preferred_element_type=F32)
    spot[...] = jnp.where(named, place, -1.0)
    counts = jnp.dot(named_f.astype(BF16), jnp.ones((256, 128), BF16), preferred_element_type=F32)
    repeat = (iota((8 * EXPERTS, EXPERTS), 0) // 8 == iota((8 * EXPERTS, EXPERTS), 1)).astype(BF16)
    count_out[...] = jnp.dot(repeat, counts.astype(BF16), preferred_element_type=F32)
    count_in[pl.ds(0, 8), :] = count_out[pl.ds(pl.multiple_of(me * 8, 8), 8), :]

    pl.semaphore_wait(barrier, EXPERTS)

    def count_copy(r):
        to = target(me, r)
        return pltpu.make_async_remote_copy(
            src_ref=count_out.at[pl.ds(pl.multiple_of(to * 8, 8), 8), :],
            dst_ref=count_in.at[pl.ds(pl.multiple_of(r * 8, 8), 8), :],
            send_sem=cnt_send.at[r],
            recv_sem=cnt_recv.at[r],
            device_id=(group, to),
            device_id_type=MESH,
        )

    def row_copy(r):
        rows = pl.ds(pl.multiple_of(r * SLOT, SLOT), SLOT)
        return pltpu.make_async_remote_copy(
            src_ref=send.at[rows, :],
            dst_ref=recv.at[rows, :],
            send_sem=send_sem.at[r],
            recv_sem=recv_sem.at[r],
            device_id=(group, target(me, r)),
            device_id_type=MESH,
        )

    def answer_copy(r):
        rows = pl.ds(pl.multiple_of(r * SLOT, SLOT), SLOT)
        return pltpu.make_async_remote_copy(
            src_ref=answer.at[rows, :],
            dst_ref=back.at[rows, :],
            send_sem=ret_send.at[r],
            recv_sem=ret_recv.at[r],
            device_id=(group, origin(me, r)),
            device_id_type=MESH,
        )

    spare_copy = pltpu.make_async_remote_copy(
        src_ref=spare_out,
        dst_ref=spare_in,
        send_sem=spare_sem.at[0],
        recv_sem=spare_sem.at[1],
        device_id=(partner, me),
        device_id_type=MESH,
    )

    @pl.loop(1, EXPERTS)
    def _(r):
        count_copy(r).start()

    loads[0].wait()
    slot_id = iota((SLOT, 256), 0).astype(F32)

    @pl.loop(0, PARTS)
    def _(b):
        blocks = []
        for j in range(PART):
            line = spot[pl.ds(target(me, b * PART + j), 1), :]
            blocks.append((line == slot_id).astype(F32))
        placer = jnp.concatenate(blocks, axis=0).astype(BF16)
        rows = pl.ds(pl.multiple_of(b * ROWS, ROWS), ROWS)
        send[rows, :] = jnp.dot(placer, tok[...], preferred_element_type=F32).astype(BF16)

        @pl.when(b == 0)
        def _():
            recv[pl.ds(0, SLOT), :] = send[pl.ds(0, SLOT), :]

        @pl.loop(0, PART)
        def _(j):
            @pl.when(b * PART + j > 0)
            def _():
                row_copy(b * PART + j).start()

    @pl.loop(0, EXPERTS)
    def _(r):
        to = target(me, r)
        line = spot[pl.ds(to, 1), :]
        weight = gate_ref[pl.ds(to // 16, 1), :]
        rows = pl.ds(pl.multiple_of(r * SLOT, SLOT), SLOT)
        scaled[rows, :] = jnp.where(line == slot_id, weight, 0.0).astype(BF16)

    @pl.loop(1, EXPERTS)
    def _(r):
        count_copy(r).wait_recv()

    arrived = count_in[...].astype(BF16)
    r_row = iota((EXPERTS, 8 * EXPERTS), 0)
    r_col = iota((EXPERTS, 8 * EXPERTS), 1)
    pick = (r_col == 8 * r_row).astype(BF16)
    before = (
        (r_col % 8 == 0) & (origin(me, r_col // 8) < origin(me, r_row))
    ).astype(BF16)
    count = jnp.dot(pick, arrived, preferred_element_type=F32)
    offset = jnp.dot(before, arrived, preferred_element_type=F32)
    limit = capacity_ref[0, 0].astype(F32)
    spare = jnp.maximum(limit - jnp.sum(count, axis=0, keepdims=True), 0.0)
    spare_out[...] = jnp.broadcast_to(spare, (8, 128))
    spare_copy.start()
    spare_copy.wait_recv()
    room = limit + jnp.minimum(spare_in[0:1, :], float(BLOCK))
    kept = jnp.minimum(jnp.maximum(room - offset, 0.0), count).astype(BF16)

    for load in loads[1:]:
        load.wait()

    @pl.loop(0, PARTS)
    def _(b):
        @pl.loop(0, PART)
        def _(j):
            @pl.when(b * PART + j > 0)
            def _():
                row_copy(b * PART + j).wait_recv()

        rows = pl.ds(pl.multiple_of(b * ROWS, ROWS), ROWS)
        own = (iota((ROWS, EXPERTS), 0) // SLOT + b * PART == iota((ROWS, EXPERTS), 1)).astype(BF16)
        most = jnp.dot(own, kept, preferred_element_type=F32)[:, 0:1]
        keep = (iota((ROWS, 1), 0) % SLOT).astype(F32) < most
        x = recv[rows, :]
        for f in range(3):
            cols = pl.ds(f * 256, 256)
            gated = jnp.dot(x, w_gate[:, cols], preferred_element_type=F32)
            upward = jnp.dot(x, w_up[:, cols], preferred_element_type=F32)
            value = gated / (1.0 + jnp.exp(-gated)) * upward
            hidden[:, cols] = jnp.where(keep, value, 0.0).astype(BF16)
        h = hidden[...]
        for d in range(4):
            cols = pl.ds(d * 512, 512)
            answer[rows, cols] = jnp.dot(
                h, w_down[:, cols], preferred_element_type=F32
            ).astype(BF16)

        @pl.when(b == 0)
        def _():
            back[pl.ds(0, SLOT), :] = answer[pl.ds(0, SLOT), :]

        @pl.loop(0, PART)
        def _(j):
            @pl.when(b * PART + j > 0)
            def _():
                answer_copy(b * PART + j).start()

    total[...] = jnp.zeros_like(total)

    @pl.loop(0, PARTS)
    def _(b):
        @pl.loop(0, PART)
        def _(j):
            @pl.when(b * PART + j > 0)
            def _():
                answer_copy(b * PART + j).wait_recv()

        rows = pl.ds(pl.multiple_of(b * ROWS, ROWS), ROWS)
        total[...] += lax.dot_general(
            scaled[rows, :], back[rows, :], (((0,), (0,)), ((), ())), preferred_element_type=F32
        )

    mixed_ref[...] = total[...].astype(BF16)

    @pl.loop(1, EXPERTS)
    def _(r):
        count_copy(r).wait_send()
        row_copy(r).wait_send()
        answer_copy(r).wait_send()

    spare_copy.wait_send()


def on_device(tokens, chosen_expert_index, routing_gate_weight, w_gate, w_up, w_down, capacity):
    rows, width = tokens.shape
    units = w_gate.shape[2]
    total_rows = EXPERTS * SLOT
    hbm = pl.BlockSpec(memory_space=pl.ANY)
    vmem = pl.BlockSpec(memory_space=pltpu.VMEM)
    smem = pl.BlockSpec(memory_space=pltpu.SMEM)
    dma = pltpu.SemaphoreType.DMA
    return pl.pallas_call(
        kernel,
        out_shape=jax.ShapeDtypeStruct((rows, width), BF16),
        in_specs=[hbm, vmem, vmem, hbm, hbm, hbm, smem],
        out_specs=vmem,
        scratch_shapes=[
            pltpu.VMEM((rows, width), BF16),
            pltpu.VMEM((width, units), BF16),
            pltpu.VMEM((width, units), BF16),
            pltpu.VMEM((units, width), BF16),
            pltpu.VMEM((total_rows, width), BF16),
            pltpu.VMEM((total_rows, width), BF16),
            pltpu.VMEM((total_rows, width), BF16),
            pltpu.VMEM((total_rows, width), BF16),
            pltpu.VMEM((EXPERTS, rows), F32),
            pltpu.VMEM((total_rows, rows), BF16),
            pltpu.VMEM((ROWS, units), BF16),
            pltpu.VMEM((rows, width), F32),
            pltpu.VMEM((8 * EXPERTS, 128), F32),
            pltpu.VMEM((8 * EXPERTS, 128), F32),
            pltpu.VMEM((8, 128), F32),
            pltpu.VMEM((8, 128), F32),
            dma((4,)),
            dma((EXPERTS,)),
            dma((EXPERTS,)),
            dma((EXPERTS,)),
            dma((EXPERTS,)),
            dma((EXPERTS,)),
            dma((EXPERTS,)),
            dma((2,)),
        ],
        compiler_params=pltpu.CompilerParams(
            collective_id=0, has_side_effects=True, vmem_limit_bytes=56 * 2**20
        ),
        cost_estimate=pl.CostEstimate(
            flops=6 * total_rows * width * units, bytes_accessed=6 * width * units, transcendentals=0
        ),
    )(
        tokens,
        chosen_expert_index[:, :8].T,
        routing_gate_weight[:, :8].T,
        w_gate,
        w_up,
        w_down,
        capacity,
    )


def solution(mesh):
    return jax.shard_map(
        on_device,
        mesh=mesh,
        in_specs=(
            P(("dp", "expert"), None),
            P(("dp", "expert"), None),
            P(("dp", "expert"), None),
            P("expert", None, None),
            P("expert", None, None),
            P("expert", None, None),
            P("dp", "expert"),
        ),
        out_specs=P(("dp", "expert"), None),
        check_vma=False,
    )
```

```python
import jax
import jax.numpy as jnp
from jax import lax
from jax.experimental import pallas as pl
from jax.experimental.pallas import tpu as pltpu
from jax.sharding import PartitionSpec as P

BLOCK = 128
SLOT = 32
EXPERTS = 32
SPLIT = 2
PIECE = SLOT // SPLIT
ROWS = 16 * PIECE
MESH = pl.DeviceIdType.MESH
F32 = jnp.float32
BF16 = jnp.bfloat16


def iota(shape, axis):
    return lax.broadcasted_iota(jnp.int32, shape, axis)


def kernel(
    tokens_hbm, index_ref, gate_ref, w_gate_hbm, w_up_hbm, w_down_hbm, capacity_ref,
    mixed_ref,
    tok, w_gate, w_up, w_down, send, relay_a, relay_b, recv, answer, home_a, home_b, back,
    spot, scaled, hidden, total, count_out, count_in, spare_out, spare_in,
    load_sem, local_sem, cnt_send, cnt_recv, spare_sem,
    a1_send, a1_recv, b1_send, b1_recv, a2_send, a2_recv, b2_send, b2_recv,
    c1_send, c1_recv, d1_send, d1_recv, c2_send, c2_recv, d2_send, d2_recv,
):
    me = lax.axis_index("expert")
    group = lax.axis_index("dp")
    groups = lax.axis_size("dp")
    partner = (group + groups // 2) % groups
    x, y, c = me // 8, (me // 2) % 4, me % 2
    half = tok.shape[1] // 2
    low, high = pl.ds(0, half), pl.ds(half, half)

    def remote(src, dst, sends, recvs, xd, yd, cd):
        return pltpu.make_async_remote_copy(
            src_ref=src,
            dst_ref=dst,
            send_sem=sends,
            recv_sem=recvs,
            device_id=(group, xd * 8 + yd * 2 + cd),
            device_id_type=MESH,
        )

    def a1(q, dx):
        xd = (x + dx) % 4
        return remote(
            send.at[q, xd, :, :, :, low], relay_a.at[q, :, :, x],
            a1_send.at[q, dx], a1_recv.at[q, dx], xd, y, c,
        )

    def b1(q, dy):
        yd = (y + dy) % 4
        return remote(
            send.at[q, :, yd, :, :, high], relay_b.at[q, :, :, y],
            b1_send.at[q, dy], b1_recv.at[q, dy], x, yd, c,
        )

    def a2(q, j):
        yd, cd = (y + j // 2) % 4, (c + j % 2) % 2
        return remote(
            relay_a.at[q, yd, cd], recv.at[q, c, y, :, :, low],
            a2_send.at[q, j], a2_recv.at[q, j], x, yd, cd,
        )

    def b2(q, j):
        xd, cd = (x + j // 2) % 4, (c + j % 2) % 2
        return remote(
            relay_b.at[q, xd, cd], recv.at[q, c, :, x, :, high],
            b2_send.at[q, j], b2_recv.at[q, j], xd, y, cd,
        )

    def c1(q, j):
        yd, cd = (y + j // 2) % 4, (c + j % 2) % 2
        return remote(
            answer.at[q, cd, yd, :, :, low], home_a.at[q, y, c],
            c1_send.at[q, j], c1_recv.at[q, j], x, yd, cd,
        )

    def d1(q, j):
        xd, cd = (x + j // 2) % 4, (c + j % 2) % 2
        return remote(
            answer.at[q, cd, :, xd, :, high], home_b.at[q, x, c],
            d1_send.at[q, j], d1_recv.at[q, j], xd, y, cd,
        )

    def c2(q, dx):
        xd = (x + dx) % 4
        return remote(
            home_a.at[q, :, :, xd], back.at[q, x, :, :, :, low],
            c2_send.at[q, dx], c2_recv.at[q, dx], xd, y, c,
        )

    def d2(q, dy):
        yd = (y + dy) % 4
        return remote(
            home_b.at[q, :, :, yd], back.at[q, :, y, :, :, high],
            d2_send.at[q, dy], d2_recv.at[q, dy], x, yd, c,
        )

    def own(q, hop):
        src, dst = [
            (send.at[q, x, :, :, :, low], relay_a.at[q, :, :, x]),
            (send.at[q, :, y, :, :, high], relay_b.at[q, :, :, y]),
            (relay_a.at[q, y, c], recv.at[q, c, y, :, :, low]),
            (relay_b.at[q, x, c], recv.at[q, c, :, x, :, high]),
            (answer.at[q, c, y, :, :, low], home_a.at[q, y, c]),
            (answer.at[q, c, :, x, :, high], home_b.at[q, x, c]),
            (home_a.at[q, :, :, x], back.at[q, x, :, :, :, low]),
            (home_b.at[q, :, :, y], back.at[q, :, y, :, :, high]),
        ][hop]
        return pltpu.make_async_copy(src, dst, local_sem.at[q, hop])

    def count_copy(r):
        to = (me + r) % EXPERTS
        return pltpu.make_async_remote_copy(
            src_ref=count_out.at[pl.ds(pl.multiple_of(to * 8, 8), 8), :],
            dst_ref=count_in.at[pl.ds(pl.multiple_of(me * 8, 8), 8), :],
            send_sem=cnt_send.at[r],
            recv_sem=cnt_recv.at[r],
            device_id=(group, to),
            device_id_type=MESH,
        )

    spare_copy = pltpu.make_async_remote_copy(
        src_ref=spare_out,
        dst_ref=spare_in,
        send_sem=spare_sem.at[0],
        recv_sem=spare_sem.at[1],
        device_id=(partner, me),
        device_id_type=MESH,
    )

    loads = [
        pltpu.make_async_copy(src, dst, load_sem.at[i])
        for i, (src, dst) in enumerate(
            [
                (tokens_hbm, tok),
                (w_gate_hbm.at[0], w_gate),
                (w_up_hbm.at[0], w_up),
                (w_down_hbm.at[0], w_down),
            ]
        )
    ]
    for load in loads:
        load.start()

    barrier = pltpu.get_barrier_semaphore()

    @pl.loop(1, EXPERTS)
    def _(r):
        pl.semaphore_signal(
            barrier, inc=1, device_id=(group, (me + r) % EXPERTS), device_id_type=MESH
        )

    pl.semaphore_signal(barrier, inc=1, device_id=(partner, me), device_id_type=MESH)

    index = index_ref[...]
    experts = iota((EXPERTS, 256), 0)
    named = (experts == index[0:1, :]) | (experts == index[1:2, :])
    named_b = named.astype(F32).astype(BF16)
    earlier = (iota((256, 256), 0) < iota((256, 256), 1)).astype(F32).astype(BF16)
    place = jnp.dot(named_b, earlier, preferred_element_type=F32)
    spot[...] = jnp.where(named, place, -1.0)
    counts = jnp.dot(named_b, jnp.ones((256, 128), BF16), preferred_element_type=F32)
    repeat = iota((8 * EXPERTS, EXPERTS), 0) // 8 == iota((8 * EXPERTS, EXPERTS), 1)
    count_out[...] = jnp.dot(
        repeat.astype(F32).astype(BF16), counts.astype(BF16), preferred_element_type=F32
    )
    mine = pl.ds(pl.multiple_of(me * 8, 8), 8)
    count_in[mine, :] = count_out[mine, :]
    loads[0].wait()

    piece_id = iota((PIECE, 256), 0)

    def pack(q):
        slot_id = (piece_id + q * PIECE).astype(F32)

        @pl.loop(0, 4)
        def _(xd):
            lines = spot[pl.ds(pl.multiple_of(xd * 8, 8), 8), :]
            placer = jnp.concatenate(
                [(lines[j : j + 1, :] == slot_id).astype(F32) for j in range(8)], axis=0
            )
            packed = jnp.dot(placer.astype(BF16), tok[...], preferred_element_type=F32)
            send[q, xd] = packed.astype(BF16).reshape(4, 2, PIECE, 2 * half)

    def start_first(q):
        @pl.loop(1, 4)
        def _(d):
            a1(q, d).start()
            b1(q, d).start()

        own(q, 0).start()
        own(q, 1).start()

    pack(0)
    pl.semaphore_wait(barrier, EXPERTS)

    @pl.loop(1, EXPERTS)
    def _(r):
        count_copy(r).start()

    start_first(0)
    pack(1)
    start_first(1)

    for q in range(SPLIT):
        slot_id = (piece_id + q * PIECE).astype(F32)

        @pl.loop(0, 4)
        def _(xd):
            lines = spot[pl.ds(pl.multiple_of(xd * 8, 8), 8), :]
            weight = gate_ref[pl.ds(xd // 2, 1), :]
            spread = jnp.concatenate(
                [jnp.where(lines[j : j + 1, :] == slot_id, weight, 0.0) for j in range(8)], axis=0
            )
            rows = pl.ds(pl.multiple_of(xd * 8 * PIECE, 8 * PIECE), 8 * PIECE)
            scaled[q, rows, :] = spread.astype(BF16)

    @pl.loop(1, EXPERTS)
    def _(r):
        count_copy(r).wait_recv()

    arrived = count_in[...].astype(BF16)
    row = iota((EXPERTS, 8 * EXPERTS), 0)
    col = iota((EXPERTS, 8 * EXPERTS), 1)
    pick = (col == 8 * row).astype(F32).astype(BF16)
    before = ((col % 8 == 0) & (col < 8 * row)).astype(F32).astype(BF16)
    count = jnp.dot(pick, arrived, preferred_element_type=F32)
    offset = jnp.dot(before, arrived, preferred_element_type=F32)
    limit = capacity_ref[0, 0].astype(F32)
    spare = jnp.maximum(limit - jnp.sum(count, axis=0, keepdims=True), 0.0)
    spare_out[...] = jnp.broadcast_to(spare, (8, 128))
    spare_copy.start()
    for q in range(SPLIT):

        @pl.loop(1, 4)
        def _(d):
            a1(q, d).wait_recv()
            b1(q, d).wait_recv()

        own(q, 0).wait()
        own(q, 1).wait()

        @pl.loop(0, 2)
        def _(dc):
            @pl.loop(0, 4)
            def _(d):
                @pl.when(d + dc > 0)
                def _():
                    a2(q, 2 * d + dc).start()
                    b2(q, 2 * d + dc).start()

        own(q, 2).start()
        own(q, 3).start()

    spare_copy.wait_recv()
    room = limit + jnp.minimum(spare_in[0:1, :], float(BLOCK))
    kept = jnp.minimum(jnp.maximum(room - offset, 0.0), count).astype(BF16)
    for load in loads[1:]:
        load.wait()

    for q in range(SPLIT):
        own(q, 2).wait()
        own(q, 3).wait()

        @pl.loop(0, 2)
        def _(dc):
            core = (c + dc) % 2

            @pl.loop(0, 4)
            def _(d):
                @pl.when(d + dc > 0)
                def _():
                    a2(q, 2 * d + dc).wait_recv()
                    b2(q, 2 * d + dc).wait_recv()

            place_id = iota((ROWS, EXPERTS), 0)
            source = (place_id // PIECE % 4) * 8 + (place_id // (4 * PIECE)) * 2 + core
            pick = (source == iota((ROWS, EXPERTS), 1)).astype(F32).astype(BF16)
            most = jnp.dot(pick, kept, preferred_element_type=F32)[:, 0:1]
            keep = (iota((ROWS, 1), 0) % PIECE + q * PIECE).astype(F32) < most
            rows = recv[q, core].reshape(ROWS, 2 * half)
            for f in range(3):
                cols = pl.ds(f * 256, 256)
                gated = jnp.dot(rows, w_gate[:, cols], preferred_element_type=F32)
                upward = jnp.dot(rows, w_up[:, cols], preferred_element_type=F32)
                value = gated / (1.0 + jnp.exp(-gated)) * upward
                hidden[:, cols] = jnp.where(keep, value, 0.0).astype(BF16)
            h = hidden[...]
            for d in range(4):
                cols = pl.ds(d * 512, 512)
                result = jnp.dot(h, w_down[:, cols], preferred_element_type=F32)
                answer[q, core, :, :, :, cols] = result.astype(BF16).reshape(4, 4, PIECE, 512)

            @pl.loop(0, 4)
            def _(d):
                @pl.when(d + dc > 0)
                def _():
                    c1(q, 2 * d + dc).start()
                    d1(q, 2 * d + dc).start()

        own(q, 4).start()
        own(q, 5).start()

    for q in range(SPLIT):

        @pl.loop(1, 8)
        def _(j):
            c1(q, j).wait_recv()
            d1(q, j).wait_recv()

        own(q, 4).wait()
        own(q, 5).wait()

        @pl.loop(1, 4)
        def _(d):
            c2(q, d).start()
            d2(q, d).start()

        own(q, 6).start()
        own(q, 7).start()

    for q in range(SPLIT):

        @pl.loop(1, 4)
        def _(d):
            c2(q, d).wait_recv()
            d2(q, d).wait_recv()

        own(q, 6).wait()
        own(q, 7).wait()
        part = lax.dot_general(
            scaled[q],
            back[q].reshape(EXPERTS * PIECE, 2 * half),
            (((0,), (0,)), ((), ())),
            preferred_element_type=F32,
        )
        if q == 0:
            total[...] = part
        else:
            mixed_ref[...] = (total[...] + part).astype(BF16)

    @pl.loop(1, EXPERTS)
    def _(r):
        count_copy(r).wait_send()

    spare_copy.wait_send()
    for q in range(SPLIT):

        @pl.loop(1, 4)
        def _(d):
            a1(q, d).wait_send()
            b1(q, d).wait_send()
            c2(q, d).wait_send()
            d2(q, d).wait_send()

        @pl.loop(1, 8)
        def _(j):
            a2(q, j).wait_send()
            b2(q, j).wait_send()
            c1(q, j).wait_send()
            d1(q, j).wait_send()


def on_device(tokens, chosen_expert_index, routing_gate_weight, w_gate, w_up, w_down, capacity):
    rows, width = tokens.shape
    units = w_gate.shape[2]
    half = width // 2
    hbm = pl.BlockSpec(memory_space=pl.ANY)
    vmem = pl.BlockSpec(memory_space=pltpu.VMEM)
    smem = pl.BlockSpec(memory_space=pltpu.SMEM)
    dma = pltpu.SemaphoreType.DMA
    wide = pltpu.VMEM((SPLIT, 4, 4, 2, PIECE, width), BF16)
    by_source = pltpu.VMEM((SPLIT, 2, 4, 4, PIECE, width), BF16)
    relay = pltpu.VMEM((SPLIT, 4, 2, 4, PIECE, half), BF16)
    near, far = dma((SPLIT, 4)), dma((SPLIT, 8))
    return pl.pallas_call(
        kernel,
        out_shape=jax.ShapeDtypeStruct((rows, width), BF16),
        in_specs=[hbm, vmem, vmem, hbm, hbm, hbm, smem],
        out_specs=vmem,
        scratch_shapes=[
            pltpu.VMEM((rows, width), BF16),
            pltpu.VMEM((width, units), BF16),
            pltpu.VMEM((width, units), BF16),
            pltpu.VMEM((units, width), BF16),
            wide,
            relay,
            relay,
            by_source,
            by_source,
            relay,
            relay,
            wide,
            pltpu.VMEM((EXPERTS, rows), F32),
            pltpu.VMEM((SPLIT, EXPERTS * PIECE, rows), BF16),
            pltpu.VMEM((ROWS, units), BF16),
            pltpu.VMEM((rows, width), F32),
            pltpu.VMEM((8 * EXPERTS, 128), F32),
            pltpu.VMEM((8 * EXPERTS, 128), F32),
            pltpu.VMEM((8, 128), F32),
            pltpu.VMEM((8, 128), F32),
            dma((4,)),
            dma((SPLIT, 8)),
            dma((EXPERTS,)),
            dma((EXPERTS,)),
            dma((2,)),
            near, near, near, near, far, far, far, far,
            far, far, far, far, near, near, near, near,
        ],
        compiler_params=pltpu.CompilerParams(
            collective_id=0, has_side_effects=True, vmem_limit_bytes=60 * 2**20
        ),
        cost_estimate=pl.CostEstimate(
            flops=6 * EXPERTS * SLOT * width * units,
            bytes_accessed=6 * width * units,
            transcendentals=0,
        ),
    )(
        tokens,
        chosen_expert_index[:, :8].T,
        routing_gate_weight[:, :8].T,
        w_gate,
        w_up,
        w_down,
        capacity,
    )


def solution(mesh):
    return jax.shard_map(
        on_device,
        mesh=mesh,
        in_specs=(
            P(("dp", "expert"), None),
            P(("dp", "expert"), None),
            P(("dp", "expert"), None),
            P("expert", None, None),
            P("expert", None, None),
            P("expert", None, None),
            P("dp", "expert"),
        ),
        out_specs=P(("dp", "expert"), None),
        check_vma=False,
    )
```

```python
import jax
import jax.numpy as jnp
from jax import lax
from jax.experimental import pallas as pl
from jax.experimental.pallas import tpu as pltpu
from jax.sharding import PartitionSpec as P

BLOCK = 128
SLOT = 32
EXPERTS = 32
SPLIT = 2
PIECE = SLOT // SPLIT
ROWS = 16 * PIECE
MESH = pl.DeviceIdType.MESH
F32 = jnp.float32
BF16 = jnp.bfloat16


def iota(shape, axis):
    return lax.broadcasted_iota(jnp.int32, shape, axis)


def kernel(
    tokens_hbm, index_ref, gate_ref, w_gate_hbm, w_up_hbm, w_down_hbm, capacity_ref,
    mixed_ref,
    tok, w_gate, w_up, w_down, send, relay_a, relay_b, recv, answer, home_a, home_b, back,
    spot, scaled, hidden, total, count_out, count_relay, count_in, spare_out, spare_mid, spare_in,
    load_sem, local_sem, cnt_sem, spare_sem, near_send, near_recv, far_send, far_recv, ret_recv,
):
    me = lax.axis_index("expert")
    group = lax.axis_index("dp")
    groups = lax.axis_size("dp")
    stride = groups // 4
    x, y, c = me // 8, (me // 2) % 4, me % 2
    half = tok.shape[1] // 2
    low, high = pl.ds(0, half), pl.ds(half, half)

    def remote(src, dst, sends, recvs, xd, yd, cd):
        return pltpu.make_async_remote_copy(
            src_ref=src,
            dst_ref=dst,
            send_sem=sends,
            recv_sem=recvs,
            device_id=(group, xd * 8 + yd * 2 + cd),
            device_id_type=MESH,
        )

    def several(ref, sem):
        return remote(ref, ref, sem, sem, x, y, 1 - c)

    def a1(q, dx):
        xd = (x + dx) % 4
        return remote(
            send.at[q, xd, :, :, low], relay_a.at[q, :, x],
            near_send.at[0], near_recv.at[0, q], xd, y, c,
        )

    def b1(q, dy):
        yd = (y + dy) % 4
        return remote(
            send.at[q, :, pl.ds(yd * 2, 2), :, high], relay_b.at[q, :, :, y],
            near_send.at[1], near_recv.at[1, q], x, yd, c,
        )

    def a2(q, d, dc):
        yd, cd = (y + d) % 4, (c + dc) % 2
        return remote(
            relay_a.at[q, yd * 2 + cd], recv.at[q, c, y, :, :, low],
            far_send.at[0], far_recv.at[0, q, dc], x, yd, cd,
        )

    def b2(q, d, dc):
        xd, cd = (x + d) % 4, (c + dc) % 2
        return remote(
            relay_b.at[q, xd, cd], recv.at[q, c, :, x, :, high],
            far_send.at[1], far_recv.at[1, q, dc], xd, y, cd,
        )

    def c1(q, d, dc):
        yd, cd = (y + d) % 4, (c + dc) % 2
        return remote(
            answer.at[q, cd, yd, :, :, low], home_a.at[q, y * 2 + c],
            far_send.at[2], ret_recv.at[0, q], x, yd, cd,
        )

    def d1(q, d, dc):
        xd, cd = (x + d) % 4, (c + dc) % 2
        return remote(
            answer.at[q, cd, :, xd, :, high], home_b.at[q, x, c],
            far_send.at[3], ret_recv.at[1, q], xd, y, cd,
        )

    def c2(q, dx):
        xd = (x + dx) % 4
        return remote(
            home_a.at[q, :, xd], back.at[q, x, :, :, low],
            near_send.at[2], near_recv.at[2, q], xd, y, c,
        )

    def d2(q, dy):
        yd = (y + dy) % 4
        return remote(
            home_b.at[q, :, :, yd], back.at[q, :, pl.ds(y * 2, 2), :, high],
            near_send.at[3], near_recv.at[3, q], x, yd, c,
        )

    def own(q, hop):
        src, dst = [
            (send.at[q, x, :, :, low], relay_a.at[q, :, x]),
            (send.at[q, :, pl.ds(y * 2, 2), :, high], relay_b.at[q, :, :, y]),
            (relay_a.at[q, y * 2 + c], recv.at[q, c, y, :, :, low]),
            (relay_b.at[q, x, c], recv.at[q, c, :, x, :, high]),
            (answer.at[q, c, y, :, :, low], home_a.at[q, y * 2 + c]),
            (answer.at[q, c, :, x, :, high], home_b.at[q, x, c]),
            (home_a.at[q, :, x], back.at[q, x, :, :, low]),
            (home_b.at[q, :, :, y], back.at[q, :, pl.ds(y * 2, 2), :, high]),
        ][hop]
        return pltpu.make_async_copy(src, dst, local_sem.at[q, hop])

    def count_near(dx):
        xd = (x + dx) % 4
        return remote(
            count_out.at[pl.ds(pl.multiple_of(xd * 8, 8), 8), :], count_relay.at[x],
            cnt_sem.at[0], cnt_sem.at[1], xd, y, c,
        )

    def count_far(j):
        return remote(
            count_relay, count_in.at[c * 4 + y],
            cnt_sem.at[2], cnt_sem.at[3], x, (y + j // 2) % 4, (c + j % 2) % 2,
        )

    def spare_copy(hop):
        src, dst = [(spare_out, spare_mid), (spare_mid, spare_in)][hop]
        return pltpu.make_async_remote_copy(
            src_ref=src,
            dst_ref=dst,
            send_sem=spare_sem.at[hop],
            recv_sem=spare_sem.at[2 + hop],
            device_id=((group + stride) % groups, me),
            device_id_type=MESH,
        )

    loads = [
        pltpu.make_async_copy(src, dst, load_sem.at[i])
        for i, (src, dst) in enumerate(
            [
                (tokens_hbm, tok),
                (w_gate_hbm.at[0], w_gate),
                (w_up_hbm.at[0], w_up),
                (w_down_hbm.at[0], w_down),
            ]
        )
    ]
    for load in loads:
        load.start()

    barrier = pltpu.get_barrier_semaphore()

    @pl.loop(1, 8)
    def _(j):
        cd = (c + j % 2) % 2
        along_y = x * 8 + (y + j // 2) % 4 * 2 + cd
        pl.semaphore_signal(barrier, inc=1, device_id=(group, along_y), device_id_type=MESH)

        @pl.when(j > 1)
        def _():
            along_x = (x + j // 2) % 4 * 8 + y * 2 + cd
            pl.semaphore_signal(barrier, inc=1, device_id=(group, along_x), device_id_type=MESH)

    for to in (stride, groups - stride):
        pl.semaphore_signal(
            barrier, inc=1, device_id=((group + to) % groups, me), device_id_type=MESH
        )

    index = index_ref[...]
    experts = iota((EXPERTS, 256), 0)
    named = (experts == index[0:1, :]) | (experts == index[1:2, :])
    named_b = named.astype(F32).astype(BF16)
    earlier = (iota((256, 256), 0) < iota((256, 256), 1)).astype(F32).astype(BF16)
    place = jnp.dot(named_b, earlier, preferred_element_type=F32)
    spot[...] = jnp.where(named, place, -1.0)
    counts = jnp.dot(named_b, jnp.ones((256, 128), BF16), preferred_element_type=F32)
    count_out[...] = counts
    count_relay[x] = count_out[pl.ds(pl.multiple_of(x * 8, 8), 8), :]
    loads[0].wait()

    piece_id = iota((PIECE, 256), 0)

    def pack(q):
        slot_id = (piece_id + q * PIECE).astype(F32)

        @pl.loop(0, 4)
        def _(xd):
            lines = spot[pl.ds(pl.multiple_of(xd * 8, 8), 8), :]
            placer = jnp.concatenate(
                [(lines[j : j + 1, :] == slot_id).astype(F32) for j in range(8)], axis=0
            )
            packed = jnp.dot(placer.astype(BF16), tok[...], preferred_element_type=F32)
            send[q, xd] = packed.astype(BF16).reshape(8, PIECE, 2 * half)

    def start_first(q):
        @pl.loop(1, 4)
        def _(d):
            a1(q, d).start()
            b1(q, d).start()

        own(q, 0).start()
        own(q, 1).start()

    pack(0)
    pl.semaphore_wait(barrier, 15)

    @pl.loop(1, 4)
    def _(d):
        count_near(d).start()

    start_first(0)
    pack(1)
    several(count_relay.at[0:3], cnt_sem.at[1]).wait_recv()

    @pl.loop(1, 8)
    def _(j):
        count_far(j).start()

    count_in[c * 4 + y] = count_relay[...]
    start_first(1)

    for q in range(SPLIT):
        slot_id = (piece_id + q * PIECE).astype(F32)

        @pl.loop(0, 4)
        def _(xd):
            lines = spot[pl.ds(pl.multiple_of(xd * 8, 8), 8), :]
            weight = gate_ref[pl.ds(xd // 2, 1), :]
            spread = jnp.concatenate(
                [jnp.where(lines[j : j + 1, :] == slot_id, weight, 0.0) for j in range(8)], axis=0
            )
            rows = pl.ds(pl.multiple_of(xd * 8 * PIECE, 8 * PIECE), 8 * PIECE)
            scaled[q, rows, :] = spread.astype(BF16)

    several(count_in.at[0:7], cnt_sem.at[3]).wait_recv()

    def place_of(r):
        return r % 4 * 8 + r // 4 % 4 * 2 + r // 16

    arrived = count_in[...].reshape(8 * EXPERTS, 128).astype(BF16)
    row = iota((EXPERTS, 8 * EXPERTS), 0)
    col = iota((EXPERTS, 8 * EXPERTS), 1)
    here = col % 8 == y * 2 + c
    pick = (here & (col // 8 == row)).astype(F32).astype(BF16)
    before = (here & (place_of(col // 8) < place_of(row))).astype(F32).astype(BF16)
    count = jnp.dot(pick, arrived, preferred_element_type=F32)
    offset = jnp.dot(before, arrived, preferred_element_type=F32)
    limit = capacity_ref[0, 0].astype(F32)
    spare = jnp.maximum(limit - jnp.sum(count, axis=0, keepdims=True), 0.0)
    spare_out[...] = jnp.broadcast_to(spare, (8, 128))
    spare_copy(0).start()
    for q in range(SPLIT):
        several(relay_a.at[q, :, 0:3], near_recv.at[0, q]).wait_recv()
        several(relay_b.at[q, :, :, 0:3], near_recv.at[1, q]).wait_recv()
        own(q, 0).wait()
        own(q, 1).wait()

        @pl.loop(0, 2)
        def _(dc):
            @pl.loop(0, 4)
            def _(d):
                @pl.when(d + dc > 0)
                def _():
                    a2(q, d, dc).start()
                    b2(q, d, dc).start()

        own(q, 2).start()
        own(q, 3).start()
        if q == 0:
            spare_copy(0).wait_recv()
            spare_copy(1).start()

    spare_copy(1).wait_recv()
    room = limit + jnp.minimum(spare_in[0:1, :], float(BLOCK))
    kept = jnp.minimum(jnp.maximum(room - offset, 0.0), count).astype(BF16)
    for load in loads[1:]:
        load.wait()

    for q in range(SPLIT):
        own(q, 2).wait()
        own(q, 3).wait()

        @pl.loop(0, 2)
        def _(dc):
            core = (c + dc) % 2

            @pl.when(dc == 0)
            def _():
                several(relay_a.at[q, 0:3], far_recv.at[0, q, 0]).wait_recv()
                several(relay_a.at[q, 0:3], far_recv.at[1, q, 0]).wait_recv()

            @pl.when(dc == 1)
            def _():
                several(relay_a.at[q, 0:4], far_recv.at[0, q, 1]).wait_recv()
                several(relay_a.at[q, 0:4], far_recv.at[1, q, 1]).wait_recv()

            source = core * 16 + iota((ROWS, EXPERTS), 0) // PIECE
            pick = (source == iota((ROWS, EXPERTS), 1)).astype(F32).astype(BF16)
            most = jnp.dot(pick, kept, preferred_element_type=F32)[:, 0:1]
            keep = (iota((ROWS, 1), 0) % PIECE + q * PIECE).astype(F32) < most
            rows = recv[q, core].reshape(ROWS, 2 * half)
            for f in range(3):
                cols = pl.ds(f * 256, 256)
                gated = jnp.dot(rows, w_gate[:, cols], preferred_element_type=F32)
                upward = jnp.dot(rows, w_up[:, cols], preferred_element_type=F32)
                value = gated / (1.0 + jnp.exp(-gated)) * upward
                hidden[:, cols] = jnp.where(keep, value, 0.0).astype(BF16)
            h = hidden[...]
            for d in range(4):
                cols = pl.ds(d * 512, 512)
                result = jnp.dot(h, w_down[:, cols], preferred_element_type=F32)
                answer[q, core, :, :, :, cols] = result.astype(BF16).reshape(4, 4, PIECE, 512)

            @pl.loop(0, 4)
            def _(d):
                @pl.when(d + dc > 0)
                def _():
                    c1(q, d, dc).start()
                    d1(q, d, dc).start()

        own(q, 4).start()
        own(q, 5).start()

    for q in range(SPLIT):
        several(relay_a.at[q, 0:7], ret_recv.at[0, q]).wait_recv()
        several(relay_a.at[q, 0:7], ret_recv.at[1, q]).wait_recv()
        own(q, 4).wait()
        own(q, 5).wait()

        @pl.loop(1, 4)
        def _(d):
            c2(q, d).start()
            d2(q, d).start()

        own(q, 6).start()
        own(q, 7).start()

    for q in range(SPLIT):
        several(relay_a.at[q, :, 0:3], near_recv.at[2, q]).wait_recv()
        several(relay_a.at[q, :, 0:3], near_recv.at[3, q]).wait_recv()
        own(q, 6).wait()
        own(q, 7).wait()
        part = lax.dot_general(
            scaled[q],
            back[q].reshape(EXPERTS * PIECE, 2 * half),
            (((0,), (0,)), ((), ())),
            preferred_element_type=F32,
        )
        if q == 0:
            total[...] = part
        else:
            mixed_ref[...] = (total[...] + part).astype(BF16)

    several(count_relay.at[0:3], cnt_sem.at[0]).wait_send()
    several(count_in.at[0:7], cnt_sem.at[2]).wait_send()
    spare_copy(0).wait_send()
    spare_copy(1).wait_send()
    for way in range(4):
        several(relay_a.at[:, :, 0:3], near_send.at[way]).wait_send()
        several(relay_a.at[:, 0:7], far_send.at[way]).wait_send()


def on_device(tokens, chosen_expert_index, routing_gate_weight, w_gate, w_up, w_down, capacity):
    rows, width = tokens.shape
    units = w_gate.shape[2]
    half = width // 2
    hbm = pl.BlockSpec(memory_space=pl.ANY)
    vmem = pl.BlockSpec(memory_space=pltpu.VMEM)
    smem = pl.BlockSpec(memory_space=pltpu.SMEM)
    dma = pltpu.SemaphoreType.DMA
    wide = pltpu.VMEM((SPLIT, 4, 8, PIECE, width), BF16)
    by_source = pltpu.VMEM((SPLIT, 2, 4, 4, PIECE, width), BF16)
    relay_a = pltpu.VMEM((SPLIT, 8, 4, PIECE, half), BF16)
    relay_b = pltpu.VMEM((SPLIT, 4, 2, 4, PIECE, half), BF16)
    return pl.pallas_call(
        kernel,
        out_shape=jax.ShapeDtypeStruct((rows, width), BF16),
        in_specs=[hbm, vmem, vmem, hbm, hbm, hbm, smem],
        out_specs=vmem,
        scratch_shapes=[
            pltpu.VMEM((rows, width), BF16),
            pltpu.VMEM((width, units), BF16),
            pltpu.VMEM((width, units), BF16),
            pltpu.VMEM((units, width), BF16),
            wide,
            relay_a,
            relay_b,
            by_source,
            by_source,
            relay_a,
            relay_b,
            wide,
            pltpu.VMEM((EXPERTS, rows), F32),
            pltpu.VMEM((SPLIT, EXPERTS * PIECE, rows), BF16),
            pltpu.VMEM((ROWS, units), BF16),
            pltpu.VMEM((rows, width), F32),
            pltpu.VMEM((EXPERTS, 128), F32),
            pltpu.VMEM((4, 8, 128), F32),
            pltpu.VMEM((8, 4, 8, 128), F32),
            pltpu.VMEM((8, 128), F32),
            pltpu.VMEM((8, 128), F32),
            pltpu.VMEM((8, 128), F32),
            dma((4,)),
            dma((SPLIT, 8)),
            dma((4,)),
            dma((4,)),
            dma((4,)),
            dma((4, SPLIT)),
            dma((4,)),
            dma((2, SPLIT, 2)),
            dma((2, SPLIT)),
        ],
        compiler_params=pltpu.CompilerParams(
            collective_id=0, has_side_effects=True, vmem_limit_bytes=60 * 2**20
        ),
        cost_estimate=pl.CostEstimate(
            flops=6 * EXPERTS * SLOT * width * units,
            bytes_accessed=6 * width * units,
            transcendentals=0,
        ),
    )(
        tokens,
        chosen_expert_index[:, :8].T,
        routing_gate_weight[:, :8].T,
        w_gate,
        w_up,
        w_down,
        capacity,
    )


def solution(mesh):
    return jax.shard_map(
        on_device,
        mesh=mesh,
        in_specs=(
            P(("dp", "expert"), None),
            P(("dp", "expert"), None),
            P(("dp", "expert"), None),
            P("expert", None, None),
            P("expert", None, None),
            P("expert", None, None),
            P("dp", "expert"),
        ),
        out_specs=P(("dp", "expert"), None),
        check_vma=False,
    )
```

```python
import jax
import jax.numpy as jnp
from jax import lax
from jax.experimental import pallas as pl
from jax.experimental.pallas import tpu as pltpu
from jax.sharding import PartitionSpec as P

BLOCK = 128
SLOT = 32
EXPERTS = 32
SPLIT = 2
PIECE = SLOT // SPLIT
ROWS = 16 * PIECE
MESH = pl.DeviceIdType.MESH
F32 = jnp.float32
BF16 = jnp.bfloat16


def iota(shape, axis):
    return lax.broadcasted_iota(jnp.int32, shape, axis)


def kernel(
    tokens_hbm, index_ref, gate_ref, w_gate_hbm, w_up_hbm, w_down_hbm, capacity_ref,
    mixed_ref,
    tok, w_gate, w_up, w_down, ring_a, ring_b, relay_a, relay_b, recv, answer, home_a, home_b, back,
    spot, spot_x, spot_y, scaled, hidden, total, count_relay, count_in, spare_out, spare_mid, spare_in,
    load_sem, local_sem, spot_sem, cnt_sem, spare_sem, ring_send, ring_recv, near_send, near_recv, far_send, far_recv, ret_recv,
):
    me = lax.axis_index("expert")
    group = lax.axis_index("dp")
    groups = lax.axis_size("dp")
    stride = groups // 4
    x, y, c = me // 8, (me // 2) % 4, me % 2
    half = tok.shape[1] // 2
    low, high = pl.ds(0, half), pl.ds(half, half)

    def remote(src, dst, sends, recvs, xd, yd, cd):
        return pltpu.make_async_remote_copy(
            src_ref=src,
            dst_ref=dst,
            send_sem=sends,
            recv_sem=recvs,
            device_id=(group, xd * 8 + yd * 2 + cd),
            device_id_type=MESH,
        )

    def several(ref, sem):
        return remote(ref, ref, sem, sem, x, y, 1 - c)

    first, second = pl.ds(0, tok.shape[0] // 2), pl.ds(tok.shape[0] // 2, tok.shape[0] // 2)

    def ring(way, order, axis):
        at, store, cols = [(x, ring_a, low), (y, ring_b, high)][axis]
        step = [1, 3][way]
        rows = [first, second] if way == 0 else [second, first]
        to = (at + step) % 4
        if order < 2:
            src, dst = tok.at[rows[order], cols], store.at[at, rows[order]]
        else:
            behind = (at + 4 - step) % 4
            src = dst = store.at[behind, rows[0]]
        return remote(
            src, dst, ring_send.at[axis], ring_recv.at[axis, way, order],
            to if axis == 0 else x, y if axis == 0 else to, c,
        )

    def spot_copy(d, axis):
        if axis == 0:
            return remote(spot, spot_x.at[x], spot_sem.at[0], spot_sem.at[1], (x + d) % 4, y, c)
        return remote(spot, spot_y.at[y], spot_sem.at[2], spot_sem.at[3], x, (y + d) % 4, c)

    def a2(q, d, dc, xs=slice(None)):
        yd, cd = (y + d) % 4, (c + dc) % 2
        return remote(
            relay_a.at[q, yd * 2 + cd, xs], recv.at[q, c, y, xs, :, low],
            far_send.at[0], far_recv.at[0, q, dc], x, yd, cd,
        )

    def b2(q, d, dc, ys=slice(None)):
        xd, cd = (x + d) % 4, (c + dc) % 2
        return remote(
            relay_b.at[q, xd, cd, ys], recv.at[q, c, ys, x, :, high],
            far_send.at[1], far_recv.at[1, q, dc], xd, y, cd,
        )

    def c1(q, d, dc):
        yd, cd = (y + d) % 4, (c + dc) % 2
        return remote(
            answer.at[q, cd, yd, :, :, low], home_a.at[q, y * 2 + c],
            far_send.at[2], ret_recv.at[0, q], x, yd, cd,
        )

    def d1(q, d, dc):
        xd, cd = (x + d) % 4, (c + dc) % 2
        return remote(
            answer.at[q, cd, :, xd, :, high], home_b.at[q, x, c],
            far_send.at[3], ret_recv.at[1, q], xd, y, cd,
        )

    def c2(q, dx):
        xd = (x + dx) % 4
        return remote(
            home_a.at[q, :, xd], back.at[q, x, :, :, low],
            near_send.at[0], near_recv.at[0, q], xd, y, c,
        )

    def d2(q, dy):
        yd = (y + dy) % 4
        return remote(
            home_b.at[q, :, :, yd], back.at[q, :, pl.ds(y * 2, 2), :, high],
            near_send.at[1], near_recv.at[1, q], x, yd, c,
        )

    def own(q, hop):
        src, dst = [
            (relay_a.at[q, y * 2 + c], recv.at[q, c, y, :, :, low]),
            (relay_b.at[q, x, c], recv.at[q, c, :, x, :, high]),
            (answer.at[q, c, y, :, :, low], home_a.at[q, y * 2 + c]),
            (answer.at[q, c, :, x, :, high], home_b.at[q, x, c]),
            (home_a.at[q, :, x], back.at[q, x, :, :, low]),
            (home_b.at[q, :, :, y], back.at[q, :, pl.ds(y * 2, 2), :, high]),
        ][hop - 2]
        return pltpu.make_async_copy(src, dst, local_sem.at[q, hop - 2])

    def count_far(j):
        return remote(
            count_relay, count_in.at[c * 4 + y],
            cnt_sem.at[0], cnt_sem.at[1], x, (y + j // 2) % 4, (c + j % 2) % 2,
        )

    def spare_copy(hop):
        src, dst = [(spare_out, spare_mid), (spare_mid, spare_in)][hop]
        return pltpu.make_async_remote_copy(
            src_ref=src,
            dst_ref=dst,
            send_sem=spare_sem.at[hop],
            recv_sem=spare_sem.at[2 + hop],
            device_id=((group + stride) % groups, me),
            device_id_type=MESH,
        )

    loads = [
        pltpu.make_async_copy(src, dst, load_sem.at[i])
        for i, (src, dst) in enumerate(
            [
                (tokens_hbm, tok),
                (w_gate_hbm.at[0], w_gate),
                (w_up_hbm.at[0], w_up),
                (w_down_hbm.at[0], w_down),
            ]
        )
    ]
    for load in loads:
        load.start()

    barrier = pltpu.get_barrier_semaphore()

    @pl.loop(1, 8)
    def _(j):
        cd = (c + j % 2) % 2
        along_y = x * 8 + (y + j // 2) % 4 * 2 + cd
        pl.semaphore_signal(barrier, inc=1, device_id=(group, along_y), device_id_type=MESH)

        @pl.when(j > 1)
        def _():
            along_x = (x + j // 2) % 4 * 8 + y * 2 + cd
            pl.semaphore_signal(barrier, inc=1, device_id=(group, along_x), device_id_type=MESH)

    for to in (stride, groups - stride):
        pl.semaphore_signal(
            barrier, inc=1, device_id=((group + to) % groups, me), device_id_type=MESH
        )

    index = index_ref[...]
    experts = iota((EXPERTS, 256), 0)
    named = (experts == index[0:1, :]) | (experts == index[1:2, :])
    named_b = named.astype(F32).astype(BF16)
    earlier = (iota((256, 256), 0) < iota((256, 256), 1)).astype(F32).astype(BF16)
    place = jnp.dot(named_b, earlier, preferred_element_type=F32)
    placed = jnp.where(named, place, -1.0)
    spot[...] = placed
    spot_x[x] = placed
    spot_y[y] = placed
    loads[0].wait()

    piece_id = iota((PIECE, 256), 0)
    pl.semaphore_wait(barrier, 15)

    @pl.loop(1, 4)
    def _(d):
        spot_copy(d, 0).start()
        spot_copy(d, 1).start()

    for order in range(2):
        for axis in range(2):
            for way in range(2):
                ring(way, order, axis).start()

    def pack(o):
        xs, ys = (x + o) % 4, (y + o) % 4
        rows_a = tok[:, low] if o == 0 else ring_a[xs]
        rows_b = tok[:, high] if o == 0 else ring_b[ys]
        lines_a = spot_x[xs, pl.ds(pl.multiple_of(x * 8, 8), 8), :]
        lines_a = [lines_a[j : j + 1, :] for j in range(8)]
        lines_b = [spot_y[ys, pl.ds(j // 2 * 8 + y * 2 + j % 2, 1), :] for j in range(8)]
        for lines, rows, side in ((lines_a, rows_a, 0), (lines_b, rows_b, 1)):
            placer = jnp.concatenate(
                [
                    (line == (piece_id + q * PIECE).astype(F32)).astype(F32)
                    for q in range(SPLIT)
                    for line in lines
                ],
                axis=0,
            )
            packed = jnp.dot(placer.astype(BF16), rows, preferred_element_type=F32).astype(BF16)
            for q in range(SPLIT):
                part = packed[q * 8 * PIECE : (q + 1) * 8 * PIECE]
                if side == 0:
                    relay_a[q, :, xs] = part.reshape(8, PIECE, half)
                else:
                    relay_b[q, :, :, ys] = part.reshape(4, 2, PIECE, half)

    def start_second(q, o):
        @pl.loop(0, 2)
        def _(dc):
            @pl.loop(0, 4)
            def _(d):
                @pl.when(d + dc > 0)
                def _():
                    if o is None:
                        a2(q, d, dc).start()
                        b2(q, d, dc).start()
                    else:
                        a2(q, d, dc, (x + o) % 4).start()
                        b2(q, d, dc, (y + o) % 4).start()

    pack(0)
    several(spot_x.at[0:3], spot_sem.at[1]).wait_recv()
    several(spot_y.at[0:3], spot_sem.at[3]).wait_recv()
    for xs in range(4):
        lines = spot_x[xs, pl.ds(pl.multiple_of(x * 8, 8), 8), :]
        number = jnp.sum((lines >= 0.0).astype(F32), axis=1, keepdims=True)
        count_relay[xs] = jnp.broadcast_to(number, (8, 128))

    @pl.loop(1, 8)
    def _(j):
        count_far(j).start()

    count_in[c * 4 + y] = count_relay[...]
    for axis in range(2):
        for way in range(2):
            ring(way, 0, axis).wait_recv()
            ring(way, 2, axis).start()

    start_second(0, 0)

    for q in range(SPLIT):
        slot_id = (piece_id + q * PIECE).astype(F32)

        @pl.loop(0, 4)
        def _(xd):
            lines = spot[pl.ds(pl.multiple_of(xd * 8, 8), 8), :]
            weight = gate_ref[pl.ds(xd // 2, 1), :]
            spread = jnp.concatenate(
                [jnp.where(lines[j : j + 1, :] == slot_id, weight, 0.0) for j in range(8)], axis=0
            )
            rows = pl.ds(pl.multiple_of(xd * 8 * PIECE, 8 * PIECE), 8 * PIECE)
            scaled[q, rows, :] = spread.astype(BF16)

    several(count_in.at[0:7], cnt_sem.at[1]).wait_recv()

    def place_of(r):
        return r % 4 * 8 + r // 4 % 4 * 2 + r // 16

    arrived = count_in[...].reshape(8 * EXPERTS, 128).astype(BF16)
    row = iota((EXPERTS, 8 * EXPERTS), 0)
    col = iota((EXPERTS, 8 * EXPERTS), 1)
    here = col % 8 == y * 2 + c
    pick = (here & (col // 8 == row)).astype(F32).astype(BF16)
    before = (here & (place_of(col // 8) < place_of(row))).astype(F32).astype(BF16)
    count = jnp.dot(pick, arrived, preferred_element_type=F32)
    offset = jnp.dot(before, arrived, preferred_element_type=F32)
    limit = capacity_ref[0, 0].astype(F32)
    spare = jnp.maximum(limit - jnp.sum(count, axis=0, keepdims=True), 0.0)
    spare_out[...] = jnp.broadcast_to(spare, (8, 128))
    spare_copy(0).start()
    for axis in range(2):
        ring(0, 1, axis).wait_recv()
    pack(3)
    start_second(0, 3)
    for axis in range(2):
        ring(1, 1, axis).wait_recv()
    pack(1)
    start_second(0, 1)
    spare_copy(0).wait_recv()
    spare_copy(1).start()
    for axis in range(2):
        for way in range(2):
            ring(way, 2, axis).wait_recv()
    pack(2)
    start_second(0, 2)
    start_second(1, None)
    for q in range(SPLIT):
        own(q, 2).start()
        own(q, 3).start()

    spare_copy(1).wait_recv()
    room = limit + jnp.minimum(spare_in[0:1, :], float(BLOCK))
    kept = jnp.minimum(jnp.maximum(room - offset, 0.0), count).astype(BF16)
    for load in loads[1:]:
        load.wait()

    for q in range(SPLIT):
        own(q, 2).wait()
        own(q, 3).wait()

        @pl.loop(0, 2)
        def _(dc):
            core = (c + dc) % 2

            @pl.when(dc == 0)
            def _():
                several(relay_a.at[q, 0:3], far_recv.at[0, q, 0]).wait_recv()
                several(relay_a.at[q, 0:3], far_recv.at[1, q, 0]).wait_recv()

            @pl.when(dc == 1)
            def _():
                several(relay_a.at[q, 0:4], far_recv.at[0, q, 1]).wait_recv()
                several(relay_a.at[q, 0:4], far_recv.at[1, q, 1]).wait_recv()

            source = core * 16 + iota((ROWS, EXPERTS), 0) // PIECE
            pick = (source == iota((ROWS, EXPERTS), 1)).astype(F32).astype(BF16)
            most = jnp.dot(pick, kept, preferred_element_type=F32)[:, 0:1]
            keep = (iota((ROWS, 1), 0) % PIECE + q * PIECE).astype(F32) < most
            rows = recv[q, core].reshape(ROWS, 2 * half)
            for f in range(3):
                cols = pl.ds(f * 256, 256)
                gated = jnp.dot(rows, w_gate[:, cols], preferred_element_type=F32)
                upward = jnp.dot(rows, w_up[:, cols], preferred_element_type=F32)
                value = gated / (1.0 + jnp.exp(-gated)) * upward
                hidden[:, cols] = jnp.where(keep, value, 0.0).astype(BF16)
            h = hidden[...]
            for d in range(4):
                cols = pl.ds(d * 512, 512)
                result = jnp.dot(h, w_down[:, cols], preferred_element_type=F32)
                answer[q, core, :, :, :, cols] = result.astype(BF16).reshape(4, 4, PIECE, 512)

            @pl.loop(0, 4)
            def _(d):
                @pl.when(d + dc > 0)
                def _():
                    c1(q, d, dc).start()
                    d1(q, d, dc).start()

        own(q, 4).start()
        own(q, 5).start()

    for q in range(SPLIT):
        several(relay_a.at[q, 0:7], ret_recv.at[0, q]).wait_recv()
        several(relay_a.at[q, 0:7], ret_recv.at[1, q]).wait_recv()
        own(q, 4).wait()
        own(q, 5).wait()

        @pl.loop(1, 4)
        def _(d):
            c2(q, d).start()
            d2(q, d).start()

        own(q, 6).start()
        own(q, 7).start()

    for q in range(SPLIT):
        several(relay_a.at[q, :, 0:3], near_recv.at[0, q]).wait_recv()
        several(relay_a.at[q, :, 0:3], near_recv.at[1, q]).wait_recv()
        own(q, 6).wait()
        own(q, 7).wait()
        part = lax.dot_general(
            scaled[q],
            back[q].reshape(EXPERTS * PIECE, 2 * half),
            (((0,), (0,)), ((), ())),
            preferred_element_type=F32,
        )
        if q == 0:
            total[...] = part
        else:
            mixed_ref[...] = (total[...] + part).astype(BF16)

    several(spot_x.at[0:3], spot_sem.at[0]).wait_send()
    several(spot_x.at[0:3], spot_sem.at[2]).wait_send()
    several(count_in.at[0:7], cnt_sem.at[0]).wait_send()
    spare_copy(0).wait_send()
    spare_copy(1).wait_send()
    for way in range(2):
        several(ring_a.at[0:3], ring_send.at[way]).wait_send()
        several(relay_a.at[:, :, 0:3], near_send.at[way]).wait_send()
    for way in range(4):
        several(relay_a.at[:, 0:7], far_send.at[way]).wait_send()


def on_device(tokens, chosen_expert_index, routing_gate_weight, w_gate, w_up, w_down, capacity):
    rows, width = tokens.shape
    units = w_gate.shape[2]
    half = width // 2
    hbm = pl.BlockSpec(memory_space=pl.ANY)
    vmem = pl.BlockSpec(memory_space=pltpu.VMEM)
    smem = pl.BlockSpec(memory_space=pltpu.SMEM)
    dma = pltpu.SemaphoreType.DMA
    wide = pltpu.VMEM((SPLIT, 4, 8, PIECE, width), BF16)
    by_source = pltpu.VMEM((SPLIT, 2, 4, 4, PIECE, width), BF16)
    relay_a = pltpu.VMEM((SPLIT, 8, 4, PIECE, half), BF16)
    relay_b = pltpu.VMEM((SPLIT, 4, 2, 4, PIECE, half), BF16)
    return pl.pallas_call(
        kernel,
        out_shape=jax.ShapeDtypeStruct((rows, width), BF16),
        in_specs=[hbm, vmem, vmem, hbm, hbm, hbm, smem],
        out_specs=vmem,
        scratch_shapes=[
            pltpu.VMEM((rows, width), BF16),
            pltpu.VMEM((width, units), BF16),
            pltpu.VMEM((width, units), BF16),
            pltpu.VMEM((units, width), BF16),
            pltpu.VMEM((4, rows, half), BF16),
            pltpu.VMEM((4, rows, half), BF16),
            relay_a,
            relay_b,
            by_source,
            by_source,
            relay_a,
            relay_b,
            wide,
            pltpu.VMEM((EXPERTS, rows), F32),
            pltpu.VMEM((4, EXPERTS, rows), F32),
            pltpu.VMEM((4, EXPERTS, rows), F32),
            pltpu.VMEM((SPLIT, EXPERTS * PIECE, rows), BF16),
            pltpu.VMEM((ROWS, units), BF16),
            pltpu.VMEM((rows, width), F32),
            pltpu.VMEM((4, 8, 128), F32),
            pltpu.VMEM((8, 4, 8, 128), F32),
            pltpu.VMEM((8, 128), F32),
            pltpu.VMEM((8, 128), F32),
            pltpu.VMEM((8, 128), F32),
            dma((4,)),
            dma((SPLIT, 6)),
            dma((4,)),
            dma((2,)),
            dma((4,)),
            dma((2,)),
            dma((2, 2, 3)),
            dma((2,)),
            dma((2, SPLIT)),
            dma((4,)),
            dma((2, SPLIT, 2)),
            dma((2, SPLIT)),
        ],
        compiler_params=pltpu.CompilerParams(
            collective_id=0, has_side_effects=True, vmem_limit_bytes=60 * 2**20
        ),
        cost_estimate=pl.CostEstimate(
            flops=6 * EXPERTS * SLOT * width * units,
            bytes_accessed=6 * width * units,
            transcendentals=0,
        ),
    )(
        tokens,
        chosen_expert_index[:, :8].T,
        routing_gate_weight[:, :8].T,
        w_gate,
        w_up,
        w_down,
        capacity,
    )


def solution(mesh):
    return jax.shard_map(
        on_device,
        mesh=mesh,
        in_specs=(
            P(("dp", "expert"), None),
            P(("dp", "expert"), None),
            P(("dp", "expert"), None),
            P("expert", None, None),
            P("expert", None, None),
            P("expert", None, None),
            P("dp", "expert"),
        ),
        out_specs=P(("dp", "expert"), None),
        check_vma=False,
    )
```

```python
import jax
import jax.numpy as jnp
from jax import lax
from jax.experimental import pallas as pl
from jax.experimental.pallas import tpu as pltpu
from jax.sharding import PartitionSpec as P

BLOCK = 128
SLOT = 32
EXPERTS = 32
SPLIT = 2
PIECE = SLOT // SPLIT
ROWS = 16 * PIECE
MESH = pl.DeviceIdType.MESH
F32 = jnp.float32
BF16 = jnp.bfloat16


def iota(shape, axis):
    return lax.broadcasted_iota(jnp.int32, shape, axis)


def kernel(
    tokens_hbm, index_ref, gate_ref, w_gate_hbm, w_up_hbm, w_down_hbm, capacity_ref,
    mixed_ref,
    tok, w_gate, w_up, w_down, ring_a, ring_b, relay_a, relay_b, recv, answer, home_a, home_b,
    sum_a, sum_b, far_a, far_b, near_a, near_b,
    spot, spot_x, spot_y, spot_a, spot_b, scaled_a, scaled_b, hidden, total, count_relay, count_in, spare_out, spare_mid, spare_in,
    load_sem, local_sem, spot_sem, cnt_sem, spare_sem, ring_send, ring_recv, sum_send, sum_recv, far_send, far_recv, ret_recv,
):
    me = lax.axis_index("expert")
    group = lax.axis_index("dp")
    groups = lax.axis_size("dp")
    stride = groups // 4
    x, y, c = me // 8, (me // 2) % 4, me % 2
    half = tok.shape[1] // 2
    low, high = pl.ds(0, half), pl.ds(half, half)

    def remote(src, dst, sends, recvs, xd, yd, cd):
        return pltpu.make_async_remote_copy(
            src_ref=src,
            dst_ref=dst,
            send_sem=sends,
            recv_sem=recvs,
            device_id=(group, xd * 8 + yd * 2 + cd),
            device_id_type=MESH,
        )

    def several(ref, sem):
        return remote(ref, ref, sem, sem, x, y, 1 - c)

    first, second = pl.ds(0, tok.shape[0] // 2), pl.ds(tok.shape[0] // 2, tok.shape[0] // 2)

    def ring(way, order, axis):
        at, store, cols = [(x, ring_a, low), (y, ring_b, high)][axis]
        step = [1, 3][way]
        rows = [first, second] if way == 0 else [second, first]
        to = (at + step) % 4
        if order < 2:
            src, dst = tok.at[rows[order], cols], store.at[at, rows[order]]
        else:
            behind = (at + 4 - step) % 4
            src = dst = store.at[behind, rows[0]]
        return remote(
            src, dst, ring_send.at[axis], ring_recv.at[axis, way, order],
            to if axis == 0 else x, y if axis == 0 else to, c,
        )

    def spot_copy(d, axis):
        if axis == 0:
            return remote(spot, spot_x.at[x], spot_sem.at[0], spot_sem.at[1], (x + d) % 4, y, c)
        return remote(spot, spot_y.at[y], spot_sem.at[2], spot_sem.at[3], x, (y + d) % 4, c)

    def a2(q, d, dc, xs=slice(None)):
        yd, cd = (y + d) % 4, (c + dc) % 2
        return remote(
            relay_a.at[q, yd * 2 + cd, xs], recv.at[q, c, y, xs, :, low],
            far_send.at[0], far_recv.at[0, q, dc], x, yd, cd,
        )

    def b2(q, d, dc, ys=slice(None)):
        xd, cd = (x + d) % 4, (c + dc) % 2
        return remote(
            relay_b.at[q, xd, cd, ys], recv.at[q, c, ys, x, :, high],
            far_send.at[1], far_recv.at[1, q, dc], xd, y, cd,
        )

    def c1(q, d, dc, o=None):
        yd, cd = (y + d) % 4, (c + dc) % 2
        xs = slice(None) if o is None else (x + o) % 4
        return remote(
            answer.at[q, cd, yd, xs, :, low], home_a.at[q, y * 2 + c, xs],
            far_send.at[2], ret_recv.at[0, 2 if o == 2 else q], x, yd, cd,
        )

    def d1(q, d, dc, o=None):
        xd, cd = (x + d) % 4, (c + dc) % 2
        ys = slice(None) if o is None else (y + o) % 4
        return remote(
            answer.at[q, cd, ys, xd, :, high], home_b.at[q, x, c, ys],
            far_send.at[3], ret_recv.at[1, 2 if o == 2 else q], xd, y, cd,
        )

    def sums(way, order, axis):
        at = [x, y][axis]
        store, far, near = [(sum_a, far_a, near_a), (sum_b, far_b, near_b)][axis]
        rows = [first, second] if way == 0 else [second, first]
        to = (at + [1, 3][way]) % 4
        if order == 0:
            src, dst = store.at[0, rows[0]], far.at[way]
        else:
            half_of = rows[2 - order]
            src, dst = store.at[1 + way, half_of], near.at[way, half_of]
        return remote(
            src, dst, sum_send.at[axis], sum_recv.at[axis, way, order],
            to if axis == 0 else x, y if axis == 0 else to, c,
        )

    def own(q, hop):
        src, dst = [
            (relay_a.at[q, y * 2 + c], recv.at[q, c, y, :, :, low]),
            (relay_b.at[q, x, c], recv.at[q, c, :, x, :, high]),
            (answer.at[q, c, y, :, :, low], home_a.at[q, y * 2 + c]),
            (answer.at[q, c, :, x, :, high], home_b.at[q, x, c]),
        ][hop - 2]
        return pltpu.make_async_copy(src, dst, local_sem.at[q, hop - 2])

    def count_far(j):
        return remote(
            count_relay, count_in.at[c * 4 + y],
            cnt_sem.at[0], cnt_sem.at[1], x, (y + j // 2) % 4, (c + j % 2) % 2,
        )

    def spare_copy(hop):
        src, dst = [(spare_out, spare_mid), (spare_mid, spare_in)][hop]
        return pltpu.make_async_remote_copy(
            src_ref=src,
            dst_ref=dst,
            send_sem=spare_sem.at[hop],
            recv_sem=spare_sem.at[2 + hop],
            device_id=((group + stride) % groups, me),
            device_id_type=MESH,
        )

    loads = [
        pltpu.make_async_copy(src, dst, load_sem.at[i])
        for i, (src, dst) in enumerate(
            [
                (tokens_hbm, tok),
                (w_gate_hbm.at[0], w_gate),
                (w_up_hbm.at[0], w_up),
                (w_down_hbm.at[0], w_down),
            ]
        )
    ]
    for load in loads:
        load.start()

    barrier = pltpu.get_barrier_semaphore()

    @pl.loop(1, 8)
    def _(j):
        cd = (c + j % 2) % 2
        along_y = x * 8 + (y + j // 2) % 4 * 2 + cd
        pl.semaphore_signal(barrier, inc=1, device_id=(group, along_y), device_id_type=MESH)

        @pl.when(j > 1)
        def _():
            along_x = (x + j // 2) % 4 * 8 + y * 2 + cd
            pl.semaphore_signal(barrier, inc=1, device_id=(group, along_x), device_id_type=MESH)

    for to in (stride, groups - stride):
        pl.semaphore_signal(
            barrier, inc=1, device_id=((group + to) % groups, me), device_id_type=MESH
        )

    index = index_ref[...]
    spot[pl.ds(0, 2), :] = index[0:2, :].astype(F32)
    spot[pl.ds(2, 2), :] = gate_ref[0:2, :]
    spot[pl.ds(4, 4), :] = jnp.zeros((4, 256), F32)
    spot_x[x] = spot[...]
    spot_y[y] = spot[...]
    earlier = (iota((256, 256), 0) < iota((256, 256), 1)).astype(F32).astype(BF16)
    loads[0].wait()

    piece_id = iota((PIECE, 256), 0)
    pl.semaphore_wait(barrier, 15)

    @pl.loop(1, 4)
    def _(d):
        spot_copy(d, 0).start()
        spot_copy(d, 1).start()

    for order in range(2):
        for axis in range(2):
            for way in range(2):
                ring(way, order, axis).start()

    def pack(o):
        xs, ys = (x + o) % 4, (y + o) % 4
        rows_a = tok[:, low] if o == 0 else ring_a[xs]
        rows_b = tok[:, high] if o == 0 else ring_b[ys]
        lines_a, lines_b = spot_a[xs], spot_b[ys]
        lines_a = [lines_a[j : j + 1, :] for j in range(8)]
        lines_b = [lines_b[j : j + 1, :] for j in range(8)]
        for lines, rows, side in ((lines_a, rows_a, 0), (lines_b, rows_b, 1)):
            placer = jnp.concatenate(
                [
                    (line == (piece_id + q * PIECE).astype(F32)).astype(F32)
                    for q in range(SPLIT)
                    for line in lines
                ],
                axis=0,
            )
            packed = jnp.dot(placer.astype(BF16), rows, preferred_element_type=F32).astype(BF16)
            for q in range(SPLIT):
                part = packed[q * 8 * PIECE : (q + 1) * 8 * PIECE]
                if side == 0:
                    relay_a[q, :, xs] = part.reshape(8, PIECE, half)
                else:
                    relay_b[q, :, :, ys] = part.reshape(4, 2, PIECE, half)

    def start_second(q, o):
        @pl.loop(0, 2)
        def _(dc):
            @pl.loop(0, 4)
            def _(d):
                @pl.when(d + dc > 0)
                def _():
                    if o is None:
                        a2(q, d, dc).start()
                        b2(q, d, dc).start()
                    else:
                        a2(q, d, dc, (x + o) % 4).start()
                        b2(q, d, dc, (y + o) % 4).start()

    several(spot_x.at[0:3], spot_sem.at[1]).wait_recv()
    several(spot_y.at[0:3], spot_sem.at[3]).wait_recv()
    j = iota((8, 256), 0)
    for store, meta, ids in ((spot_a, spot_x, x * 8 + j), (spot_b, spot_y, j // 2 * 8 + y * 2 + j % 2)):
        ids = ids.astype(F32)
        named = jnp.concatenate(
            [
                ((meta[at, 0:1, :] == ids) | (meta[at, 1:2, :] == ids)).astype(F32)
                for at in range(4)
            ],
            axis=0,
        )
        place = jnp.dot(named.astype(BF16), earlier, preferred_element_type=F32)
        store[...] = jnp.where(named > 0.0, place, -1.0).reshape(4, 8, 256)
    for xs in range(4):
        number = jnp.sum((spot_a[xs] >= 0.0).astype(F32), axis=1, keepdims=True)
        count_relay[xs] = jnp.broadcast_to(number, (8, 128))

    @pl.loop(1, 8)
    def _(j):
        count_far(j).start()

    count_in[c * 4 + y] = count_relay[...]
    pack(0)
    for axis in range(2):
        for way in range(2):
            ring(way, 0, axis).wait_recv()
            ring(way, 2, axis).start()

    start_second(0, 0)

    @pl.loop(0, 4)
    def _(at):
        lines_a, lines_b = spot_a[at], spot_b[at]
        weight_a = spot_x[at, pl.ds(2 + x // 2, 1), :]
        for j in range(8):
            line_b = lines_b[j : j + 1, :]
            weight_b = spot_y[at, pl.ds(2 + j // 4, 1), :]
            for q in range(SPLIT):
                slot_id = (piece_id + q * PIECE).astype(F32)
                rows = pl.ds(j * PIECE, PIECE)
                spread = jnp.where(lines_a[j : j + 1, :] == slot_id, weight_a, 0.0)
                scaled_a[at, q, rows, :] = spread.astype(BF16)
                spread = jnp.where(line_b == slot_id, weight_b, 0.0)
                scaled_b[at, q, rows, :] = spread.astype(BF16)

    several(count_in.at[0:7], cnt_sem.at[1]).wait_recv()

    def place_of(r):
        return r % 4 * 8 + r // 4 % 4 * 2 + r // 16

    arrived = count_in[...].reshape(8 * EXPERTS, 128).astype(BF16)
    row = iota((EXPERTS, 8 * EXPERTS), 0)
    col = iota((EXPERTS, 8 * EXPERTS), 1)
    here = col % 8 == y * 2 + c
    pick = (here & (col // 8 == row)).astype(F32).astype(BF16)
    before = (here & (place_of(col // 8) < place_of(row))).astype(F32).astype(BF16)
    count = jnp.dot(pick, arrived, preferred_element_type=F32)
    offset = jnp.dot(before, arrived, preferred_element_type=F32)
    limit = capacity_ref[0, 0].astype(F32)
    spare = jnp.maximum(limit - jnp.sum(count, axis=0, keepdims=True), 0.0)
    spare_out[...] = jnp.broadcast_to(spare, (8, 128))
    spare_copy(0).start()
    for axis in range(2):
        ring(0, 1, axis).wait_recv()
    pack(3)
    start_second(0, 3)
    for axis in range(2):
        ring(1, 1, axis).wait_recv()
    pack(1)
    start_second(0, 1)
    spare_copy(0).wait_recv()
    spare_copy(1).start()
    for axis in range(2):
        for way in range(2):
            ring(way, 2, axis).wait_recv()
    pack(2)
    start_second(0, 2)
    start_second(1, None)
    for q in range(SPLIT):
        own(q, 2).start()
        own(q, 3).start()

    spare_copy(1).wait_recv()
    room = limit + jnp.minimum(spare_in[0:1, :], float(BLOCK))
    kept = jnp.minimum(jnp.maximum(room - offset, 0.0), count).astype(BF16)
    for load in loads[1:]:
        load.wait()

    for q in range(SPLIT):
        own(q, 2).wait()
        own(q, 3).wait()

        @pl.loop(0, 2)
        def _(dc):
            core = (c + dc) % 2

            @pl.when(dc == 0)
            def _():
                several(relay_a.at[q, 0:3], far_recv.at[0, q, 0]).wait_recv()
                several(relay_a.at[q, 0:3], far_recv.at[1, q, 0]).wait_recv()

            @pl.when(dc == 1)
            def _():
                several(relay_a.at[q, 0:4], far_recv.at[0, q, 1]).wait_recv()
                several(relay_a.at[q, 0:4], far_recv.at[1, q, 1]).wait_recv()

            source = core * 16 + iota((ROWS, EXPERTS), 0) // PIECE
            pick = (source == iota((ROWS, EXPERTS), 1)).astype(F32).astype(BF16)
            most = jnp.dot(pick, kept, preferred_element_type=F32)[:, 0:1]
            keep = (iota((ROWS, 1), 0) % PIECE + q * PIECE).astype(F32) < most
            rows = recv[q, core].reshape(ROWS, 2 * half)
            for f in range(3):
                cols = pl.ds(f * 256, 256)
                gated = jnp.dot(rows, w_gate[:, cols], preferred_element_type=F32)
                upward = jnp.dot(rows, w_up[:, cols], preferred_element_type=F32)
                value = gated / (1.0 + jnp.exp(-gated)) * upward
                hidden[:, cols] = jnp.where(keep, value, 0.0).astype(BF16)
            h = hidden[...]
            for d in range(4):
                cols = pl.ds(d * 512, 512)
                result = jnp.dot(h, w_down[:, cols], preferred_element_type=F32)
                answer[q, core, :, :, :, cols] = result.astype(BF16).reshape(4, 4, PIECE, 512)

            for o in (None,) if q == 0 else (2, 1, 3, 0):

                @pl.loop(0, 4)
                def _(d):
                    @pl.when(d + dc > 0)
                    def _():
                        c1(q, d, dc, o).start()
                        d1(q, d, dc, o).start()

        own(q, 4).start()
        own(q, 5).start()

    for q in range(SPLIT):
        own(q, 4).wait()
        own(q, 5).wait()
    for axis in range(2):
        several(relay_a.at[0, 0:7], ret_recv.at[axis, 0]).wait_recv()
        several(relay_a.at[0, 0:7, 0], ret_recv.at[axis, 2]).wait_recv()

    def sum_for(o, axis):
        at = ([x, y][axis] + o) % 4
        result = None
        for q in range(SPLIT):
            rows = home_a[q, :, at] if axis == 0 else home_b[q, :, :, at]
            share = lax.dot_general(
                (scaled_a if axis == 0 else scaled_b)[at, q],
                rows.reshape(8 * PIECE, half),
                (((0,), (0,)), ((), ())),
                preferred_element_type=F32,
            )
            result = share if result is None else result + share
        return result

    for axis in range(2):
        store = [sum_a, sum_b][axis]
        store[0] = sum_for(2, axis).astype(BF16)
        for way in range(2):
            sums(way, 0, axis).start()
    for axis in range(2):
        several(relay_a.at[0, 0:7, 0:3], ret_recv.at[axis, 1]).wait_recv()
    for way in range(2):
        for axis in range(2):
            store = [sum_a, sum_b][axis]
            store[1 + way] = sum_for([1, 3][way], axis).astype(BF16)
            sums(way, 1, axis).start()
    for axis in range(2):
        total[:, [low, high][axis]] = sum_for(0, axis)
    for way in range(2):
        for axis in range(2):
            store, far = [(sum_a, far_a), (sum_b, far_b)][axis]
            rows = [first, second][way]
            sums(way, 0, axis).wait_recv()
            merged = store[1 + way, rows, :].astype(F32) + far[way].astype(F32)
            store[1 + way, rows, :] = merged.astype(BF16)
            sums(way, 2, axis).start()
    for order in (1, 2):
        for axis in range(2):
            near, cols = [(near_a, low), (near_b, high)][axis]
            for way in range(2):
                sums(way, order, axis).wait_recv()
                rows = [first, second][way if order == 2 else 1 - way]
                total[rows, cols] += near[way, rows, :].astype(F32)
    mixed_ref[...] = total[...].astype(BF16)

    several(spot_x.at[0:3], spot_sem.at[0]).wait_send()
    several(spot_x.at[0:3], spot_sem.at[2]).wait_send()
    several(count_in.at[0:7], cnt_sem.at[0]).wait_send()
    spare_copy(0).wait_send()
    spare_copy(1).wait_send()
    for way in range(2):
        several(ring_a.at[0:3], ring_send.at[way]).wait_send()
        several(ring_a.at[0:3], sum_send.at[way]).wait_send()
    for way in range(4):
        several(relay_a.at[:, 0:7], far_send.at[way]).wait_send()


def on_device(tokens, chosen_expert_index, routing_gate_weight, w_gate, w_up, w_down, capacity):
    rows, width = tokens.shape
    units = w_gate.shape[2]
    half = width // 2
    hbm = pl.BlockSpec(memory_space=pl.ANY)
    vmem = pl.BlockSpec(memory_space=pltpu.VMEM)
    smem = pl.BlockSpec(memory_space=pltpu.SMEM)
    dma = pltpu.SemaphoreType.DMA
    per_token = pltpu.VMEM((4, SPLIT, 8 * PIECE, rows), BF16)
    by_source = pltpu.VMEM((SPLIT, 2, 4, 4, PIECE, width), BF16)
    relay_a = pltpu.VMEM((SPLIT, 8, 4, PIECE, half), BF16)
    relay_b = pltpu.VMEM((SPLIT, 4, 2, 4, PIECE, half), BF16)
    return pl.pallas_call(
        kernel,
        out_shape=jax.ShapeDtypeStruct((rows, width), BF16),
        in_specs=[hbm, vmem, vmem, hbm, hbm, hbm, smem],
        out_specs=vmem,
        scratch_shapes=[
            pltpu.VMEM((rows, width), BF16),
            pltpu.VMEM((width, units), BF16),
            pltpu.VMEM((width, units), BF16),
            pltpu.VMEM((units, width), BF16),
            pltpu.VMEM((4, rows, half), BF16),
            pltpu.VMEM((4, rows, half), BF16),
            relay_a,
            relay_b,
            by_source,
            by_source,
            relay_a,
            relay_b,
            pltpu.VMEM((3, rows, half), BF16),
            pltpu.VMEM((3, rows, half), BF16),
            pltpu.VMEM((2, rows // 2, half), BF16),
            pltpu.VMEM((2, rows // 2, half), BF16),
            pltpu.VMEM((2, rows, half), BF16),
            pltpu.VMEM((2, rows, half), BF16),
            pltpu.VMEM((8, rows), F32),
            pltpu.VMEM((4, 8, rows), F32),
            pltpu.VMEM((4, 8, rows), F32),
            pltpu.VMEM((4, 8, rows), F32),
            pltpu.VMEM((4, 8, rows), F32),
            per_token,
            per_token,
            pltpu.VMEM((ROWS, units), BF16),
            pltpu.VMEM((rows, width), F32),
            pltpu.VMEM((4, 8, 128), F32),
            pltpu.VMEM((8, 4, 8, 128), F32),
            pltpu.VMEM((8, 128), F32),
            pltpu.VMEM((8, 128), F32),
            pltpu.VMEM((8, 128), F32),
            dma((4,)),
            dma((SPLIT, 4)),
            dma((4,)),
            dma((2,)),
            dma((4,)),
            dma((2,)),
            dma((2, 2, 3)),
            dma((2,)),
            dma((2, 2, 3)),
            dma((4,)),
            dma((2, SPLIT, 2)),
            dma((2, SPLIT + 1)),
        ],
        compiler_params=pltpu.CompilerParams(
            collective_id=0, has_side_effects=True, vmem_limit_bytes=60 * 2**20
        ),
        cost_estimate=pl.CostEstimate(
            flops=6 * EXPERTS * SLOT * width * units,
            bytes_accessed=6 * width * units,
            transcendentals=0,
        ),
    )(
        tokens,
        chosen_expert_index[:, :8].T,
        routing_gate_weight[:, :8].T,
        w_gate,
        w_up,
        w_down,
        capacity,
    )


def solution(mesh):
    return jax.shard_map(
        on_device,
        mesh=mesh,
        in_specs=(
            P(("dp", "expert"), None),
            P(("dp", "expert"), None),
            P(("dp", "expert"), None),
            P("expert", None, None),
            P("expert", None, None),
            P("expert", None, None),
            P("dp", "expert"),
        ),
        out_specs=P(("dp", "expert"), None),
        check_vma=False,
    )
```

```python
import jax
import jax.numpy as jnp
from jax import lax
from jax.experimental import pallas as pl
from jax.experimental.pallas import tpu as pltpu
from jax.sharding import PartitionSpec as P

BLOCK = 128
SLOT = 32
EXPERTS = 32
SPLIT = 2
PIECE = SLOT // SPLIT
ROWS = 16 * PIECE
MESH = pl.DeviceIdType.MESH
F32 = jnp.float32
BF16 = jnp.bfloat16


def iota(shape, axis):
    return lax.broadcasted_iota(jnp.int32, shape, axis)


def kernel(
    tokens_hbm, index_ref, gate_ref, w_gate_hbm, w_up_hbm, w_down_hbm, capacity_ref,
    mixed_ref,
    tok, w_gate, w_up, w_down, ring_a, ring_b, relay_a, relay_b, recv, answer, home_a, home_b,
    sum_a, sum_b, far_a, far_b, near_a, near_b,
    spot, spot_x, spot_y, spot_a, spot_b, scaled_a, scaled_b, hidden, total, count_relay, count_in, spare_out, spare_mid, spare_in,
    load_sem, local_sem, spot_sem, cnt_sem, spare_sem, ring_send, ring_recv, sum_send, sum_recv, far_send, far_recv, ret_recv,
):
    me = lax.axis_index("expert")
    group = lax.axis_index("dp")
    groups = lax.axis_size("dp")
    stride = groups // 4
    x, y, c = me // 8, (me // 2) % 4, me % 2
    half = tok.shape[1] // 2
    low, high = pl.ds(0, half), pl.ds(half, half)

    def remote(src, dst, sends, recvs, xd, yd, cd):
        return pltpu.make_async_remote_copy(
            src_ref=src,
            dst_ref=dst,
            send_sem=sends,
            recv_sem=recvs,
            device_id=(group, xd * 8 + yd * 2 + cd),
            device_id_type=MESH,
        )

    def several(ref, sem):
        return remote(ref, ref, sem, sem, x, y, 1 - c)

    first, second = pl.ds(0, tok.shape[0] // 2), pl.ds(tok.shape[0] // 2, tok.shape[0] // 2)

    def ring(way, order, axis):
        at, store, cols = [(x, ring_a, low), (y, ring_b, high)][axis]
        step = [1, 3][way]
        rows = [first, second] if way == 0 else [second, first]
        to = (at + step) % 4
        if order < 2:
            src, dst = tok.at[rows[order], cols], store.at[at, rows[order]]
        else:
            behind = (at + 4 - step) % 4
            src = dst = store.at[behind, rows[0]]
        return remote(
            src, dst, ring_send.at[axis], ring_recv.at[axis, way, order],
            to if axis == 0 else x, y if axis == 0 else to, c,
        )

    def spot_copy(d, axis):
        if axis == 0:
            return remote(spot, spot_x.at[x], spot_sem.at[0], spot_sem.at[1], (x + d) % 4, y, c)
        return remote(spot, spot_y.at[y], spot_sem.at[2], spot_sem.at[3], x, (y + d) % 4, c)

    def a2(q, d, dc, xs=slice(None)):
        yd, cd = (y + d) % 4, (c + dc) % 2
        return remote(
            relay_a.at[q, yd * 2 + cd, xs], recv.at[q, c, y, xs, :, low],
            far_send.at[0], far_recv.at[0, q, dc], x, yd, cd,
        )

    def b2(q, d, dc, ys=slice(None)):
        xd, cd = (x + d) % 4, (c + dc) % 2
        return remote(
            relay_b.at[q, xd, cd, ys], recv.at[q, c, ys, x, :, high],
            far_send.at[1], far_recv.at[1, q, dc], xd, y, cd,
        )

    def c1(q, d, dc, o=None):
        yd, cd = (y + d) % 4, (c + dc) % 2
        xs = slice(None) if o is None else (x + o) % 4
        return remote(
            answer.at[q, cd, yd, xs, :, low], home_a.at[q, y * 2 + c, xs],
            far_send.at[2], ret_recv.at[0, q if o is None else 2 if o == 2 else 3 if o == 0 else 1], x, yd, cd,
        )

    def d1(q, d, dc, o=None):
        xd, cd = (x + d) % 4, (c + dc) % 2
        ys = slice(None) if o is None else (y + o) % 4
        return remote(
            answer.at[q, cd, ys, xd, :, high], home_b.at[q, x, c, ys],
            far_send.at[3], ret_recv.at[1, q if o is None else 2 if o == 2 else 3 if o == 0 else 1], xd, y, cd,
        )

    def sums(way, order, axis):
        at = [x, y][axis]
        store, far, near = [(sum_a, far_a, near_a), (sum_b, far_b, near_b)][axis]
        rows = [first, second] if way == 0 else [second, first]
        to = (at + [1, 3][way]) % 4
        if order == 0:
            src, dst = store.at[0, rows[0]], far.at[way]
        else:
            half_of = rows[2 - order]
            src, dst = store.at[1 + way, half_of], near.at[way, half_of]
        return remote(
            src, dst, sum_send.at[axis], sum_recv.at[axis, way, order],
            to if axis == 0 else x, y if axis == 0 else to, c,
        )

    def own(q, hop):
        src, dst = [
            (relay_a.at[q, y * 2 + c], recv.at[q, c, y, :, :, low]),
            (relay_b.at[q, x, c], recv.at[q, c, :, x, :, high]),
            (answer.at[q, c, y, :, :, low], home_a.at[q, y * 2 + c]),
            (answer.at[q, c, :, x, :, high], home_b.at[q, x, c]),
        ][hop - 2]
        return pltpu.make_async_copy(src, dst, local_sem.at[q, hop - 2])

    def count_far(j):
        return remote(
            count_relay, count_in.at[c * 4 + y],
            cnt_sem.at[0], cnt_sem.at[1], x, (y + j // 2) % 4, (c + j % 2) % 2,
        )

    def spare_copy(hop):
        src, dst = [(spare_out, spare_mid), (spare_mid, spare_in)][hop]
        return pltpu.make_async_remote_copy(
            src_ref=src,
            dst_ref=dst,
            send_sem=spare_sem.at[hop],
            recv_sem=spare_sem.at[2 + hop],
            device_id=((group + stride) % groups, me),
            device_id_type=MESH,
        )

    loads = [
        pltpu.make_async_copy(src, dst, load_sem.at[i])
        for i, (src, dst) in enumerate(
            [
                (tokens_hbm, tok),
                (w_gate_hbm.at[0], w_gate),
                (w_up_hbm.at[0], w_up),
                (w_down_hbm.at[0], w_down),
            ]
        )
    ]
    for load in loads:
        load.start()

    barrier = pltpu.get_barrier_semaphore()

    @pl.loop(1, 8)
    def _(j):
        cd = (c + j % 2) % 2
        along_y = x * 8 + (y + j // 2) % 4 * 2 + cd
        pl.semaphore_signal(barrier, inc=1, device_id=(group, along_y), device_id_type=MESH)

        @pl.when(j > 1)
        def _():
            along_x = (x + j // 2) % 4 * 8 + y * 2 + cd
            pl.semaphore_signal(barrier, inc=1, device_id=(group, along_x), device_id_type=MESH)

    for to in (stride, groups - stride):
        pl.semaphore_signal(
            barrier, inc=1, device_id=((group + to) % groups, me), device_id_type=MESH
        )

    index = index_ref[...]
    spot[pl.ds(0, 2), :] = index[0:2, :].astype(F32)
    spot[pl.ds(2, 2), :] = gate_ref[0:2, :]
    spot[pl.ds(4, 4), :] = jnp.zeros((4, 256), F32)
    spot_x[x] = spot[...]
    spot_y[y] = spot[...]
    earlier = (iota((256, 256), 0) < iota((256, 256), 1)).astype(F32).astype(BF16)
    loads[0].wait()

    piece_id = iota((PIECE, 256), 0)
    pl.semaphore_wait(barrier, 15)

    @pl.loop(1, 4)
    def _(d):
        spot_copy(d, 0).start()
        spot_copy(d, 1).start()

    for order in range(2):
        for axis in range(2):
            for way in range(2):
                ring(way, order, axis).start()

    def pack(o):
        xs, ys = (x + o) % 4, (y + o) % 4
        rows_a = tok[:, low] if o == 0 else ring_a[xs]
        rows_b = tok[:, high] if o == 0 else ring_b[ys]
        lines_a, lines_b = spot_a[xs], spot_b[ys]
        lines_a = [lines_a[j : j + 1, :] for j in range(8)]
        lines_b = [lines_b[j : j + 1, :] for j in range(8)]
        for lines, rows, side in ((lines_a, rows_a, 0), (lines_b, rows_b, 1)):
            placer = jnp.concatenate(
                [
                    (line == (piece_id + q * PIECE).astype(F32)).astype(F32)
                    for q in range(SPLIT)
                    for line in lines
                ],
                axis=0,
            )
            packed = jnp.dot(placer.astype(BF16), rows, preferred_element_type=F32).astype(BF16)
            for q in range(SPLIT):
                part = packed[q * 8 * PIECE : (q + 1) * 8 * PIECE]
                if side == 0:
                    relay_a[q, :, xs] = part.reshape(8, PIECE, half)
                else:
                    relay_b[q, :, :, ys] = part.reshape(4, 2, PIECE, half)

    def start_second(q, o):
        @pl.loop(0, 2)
        def _(dc):
            @pl.loop(0, 4)
            def _(d):
                @pl.when(d + dc > 0)
                def _():
                    if o is None:
                        a2(q, d, dc).start()
                        b2(q, d, dc).start()
                    else:
                        a2(q, d, dc, (x + o) % 4).start()
                        b2(q, d, dc, (y + o) % 4).start()

    several(spot_x.at[0:3], spot_sem.at[1]).wait_recv()
    several(spot_y.at[0:3], spot_sem.at[3]).wait_recv()
    j = iota((8, 256), 0)
    for store, meta, ids in ((spot_a, spot_x, x * 8 + j), (spot_b, spot_y, j // 2 * 8 + y * 2 + j % 2)):
        ids = ids.astype(F32)
        named = jnp.concatenate(
            [
                ((meta[at, 0:1, :] == ids) | (meta[at, 1:2, :] == ids)).astype(F32)
                for at in range(4)
            ],
            axis=0,
        )
        place = jnp.dot(named.astype(BF16), earlier, preferred_element_type=F32)
        store[...] = jnp.where(named > 0.0, place, -1.0).reshape(4, 8, 256)
    lane = iota((8, 128), 1)
    numbers = jnp.zeros((8, 128), F32)
    for xs in range(4):
        number = jnp.sum((spot_a[xs] >= 0.0).astype(F32), axis=1, keepdims=True)
        numbers = jnp.where(lane == xs, number, numbers)
    count_relay[...] = numbers

    @pl.loop(1, 8)
    def _(j):
        count_far(j).start()

    count_in[c * 4 + y] = count_relay[...]
    pack(0)
    for axis in range(2):
        for way in range(2):
            ring(way, 0, axis).wait_recv()
            ring(way, 2, axis).start()

    start_second(0, 0)

    @pl.loop(0, 4)
    def _(at):
        lines_a, lines_b = spot_a[at], spot_b[at]
        weight_a = spot_x[at, pl.ds(2 + x // 2, 1), :]
        for j in range(8):
            line_b = lines_b[j : j + 1, :]
            weight_b = spot_y[at, pl.ds(2 + j // 4, 1), :]
            for q in range(SPLIT):
                slot_id = (piece_id + q * PIECE).astype(F32)
                rows = pl.ds(j * PIECE, PIECE)
                spread = jnp.where(lines_a[j : j + 1, :] == slot_id, weight_a, 0.0)
                scaled_a[at, q, rows, :] = spread.astype(BF16)
                spread = jnp.where(line_b == slot_id, weight_b, 0.0)
                scaled_b[at, q, rows, :] = spread.astype(BF16)

    several(count_in.at[0:7], cnt_sem.at[1]).wait_recv()

    def place_of(r):
        return r % 4 * 8 + r // 4 % 4 * 2 + r // 16

    arrived = count_in[...].reshape(2 * EXPERTS, 128).astype(BF16)
    row, col = iota((EXPERTS, 2 * EXPERTS), 0), iota((EXPERTS, 2 * EXPERTS), 1)
    pick = (col == row // 4 * 8 + y * 2 + c).astype(F32).astype(BF16)
    by_lane = jnp.dot(pick, arrived, preferred_element_type=F32)
    chosen = iota((EXPERTS, 128), 1) == iota((EXPERTS, 128), 0) % 4
    count = jnp.sum(jnp.where(chosen, by_lane, 0.0), axis=1, keepdims=True)
    count = jnp.broadcast_to(count, (EXPERTS, 128))
    row, col = iota((EXPERTS, EXPERTS), 0), iota((EXPERTS, EXPERTS), 1)
    before = (place_of(col) < place_of(row)).astype(F32).astype(BF16)
    offset = jnp.dot(before, count.astype(BF16), preferred_element_type=F32)
    limit = capacity_ref[0, 0].astype(F32)
    spare = jnp.maximum(limit - jnp.sum(count, axis=0, keepdims=True), 0.0)
    spare_out[...] = jnp.broadcast_to(spare, (8, 128))
    spare_copy(0).start()
    for axis in range(2):
        ring(0, 1, axis).wait_recv()
    pack(3)
    start_second(0, 3)
    for axis in range(2):
        ring(1, 1, axis).wait_recv()
    pack(1)
    start_second(0, 1)
    spare_copy(0).wait_recv()
    spare_copy(1).start()
    for axis in range(2):
        for way in range(2):
            ring(way, 2, axis).wait_recv()
    pack(2)
    start_second(0, 2)
    start_second(1, None)
    for q in range(SPLIT):
        own(q, 2).start()
        own(q, 3).start()

    spare_copy(1).wait_recv()
    room = limit + jnp.minimum(spare_in[0:1, :], float(BLOCK))
    kept = jnp.minimum(jnp.maximum(room - offset, 0.0), count).astype(BF16)
    for load in loads[1:]:
        load.wait()

    for q in range(SPLIT):
        own(q, 2).wait()
        own(q, 3).wait()

        @pl.loop(0, 2)
        def _(dc):
            core = (c + dc) % 2

            @pl.when(dc == 0)
            def _():
                several(relay_a.at[q, 0:3], far_recv.at[0, q, 0]).wait_recv()
                several(relay_a.at[q, 0:3], far_recv.at[1, q, 0]).wait_recv()

            @pl.when(dc == 1)
            def _():
                several(relay_a.at[q, 0:4], far_recv.at[0, q, 1]).wait_recv()
                several(relay_a.at[q, 0:4], far_recv.at[1, q, 1]).wait_recv()

            source = core * 16 + iota((ROWS, EXPERTS), 0) // PIECE
            pick = (source == iota((ROWS, EXPERTS), 1)).astype(F32).astype(BF16)
            most = jnp.dot(pick, kept, preferred_element_type=F32)[:, 0:1]
            keep = (iota((ROWS, 1), 0) % PIECE + q * PIECE).astype(F32) < most
            rows = recv[q, core].reshape(ROWS, 2 * half)
            for f in range(3):
                cols = pl.ds(f * 256, 256)
                gated = jnp.dot(rows, w_gate[:, cols], preferred_element_type=F32)
                upward = jnp.dot(rows, w_up[:, cols], preferred_element_type=F32)
                value = gated / (1.0 + jnp.exp(-gated)) * upward
                hidden[:, cols] = jnp.where(keep, value, 0.0).astype(BF16)
            h = hidden[...]
            for d in range(4):
                cols = pl.ds(d * 512, 512)
                result = jnp.dot(h, w_down[:, cols], preferred_element_type=F32)
                answer[q, core, :, :, :, cols] = result.astype(BF16).reshape(4, 4, PIECE, 512)

            for o in (None,) if q == 0 else (2,):

                @pl.loop(0, 4)
                def _(d):
                    @pl.when(d + dc > 0)
                    def _():
                        c1(q, d, dc, o).start()
                        d1(q, d, dc, o).start()

        if q == SPLIT - 1:
            for o in (1, 3, 0):

                @pl.loop(1, 8)
                def _(j):
                    c1(q, j // 2, j % 2, o).start()
                    d1(q, j // 2, j % 2, o).start()

        own(q, 4).start()
        own(q, 5).start()

    for q in range(SPLIT):
        own(q, 4).wait()
        own(q, 5).wait()
    for axis in range(2):
        several(relay_a.at[0, 0:7], ret_recv.at[axis, 0]).wait_recv()
        several(relay_a.at[0, 0:7, 0], ret_recv.at[axis, 2]).wait_recv()

    def sum_for(o, axis):
        at = ([x, y][axis] + o) % 4
        result = None
        for q in range(SPLIT):
            rows = home_a[q, :, at] if axis == 0 else home_b[q, :, :, at]
            share = lax.dot_general(
                (scaled_a if axis == 0 else scaled_b)[at, q],
                rows.reshape(8 * PIECE, half),
                (((0,), (0,)), ((), ())),
                preferred_element_type=F32,
            )
            result = share if result is None else result + share
        return result

    for axis in range(2):
        store = [sum_a, sum_b][axis]
        store[0] = sum_for(2, axis).astype(BF16)
        for way in range(2):
            sums(way, 0, axis).start()
    for axis in range(2):
        several(relay_a.at[0, 0:7, 0:2], ret_recv.at[axis, 1]).wait_recv()
    for way in range(2):
        for axis in range(2):
            store = [sum_a, sum_b][axis]
            store[1 + way] = sum_for([1, 3][way], axis).astype(BF16)
            sums(way, 1, axis).start()
    for axis in range(2):
        several(relay_a.at[0, 0:7, 0], ret_recv.at[axis, 3]).wait_recv()
        total[:, [low, high][axis]] = sum_for(0, axis)
    for way in range(2):
        for axis in range(2):
            store, far = [(sum_a, far_a), (sum_b, far_b)][axis]
            rows = [first, second][way]
            sums(way, 0, axis).wait_recv()
            merged = store[1 + way, rows, :].astype(F32) + far[way].astype(F32)
            store[1 + way, rows, :] = merged.astype(BF16)
            sums(way, 2, axis).start()
    for order in (1, 2):
        for axis in range(2):
            near, cols = [(near_a, low), (near_b, high)][axis]
            for way in range(2):
                sums(way, order, axis).wait_recv()
                rows = [first, second][way if order == 2 else 1 - way]
                total[rows, cols] += near[way, rows, :].astype(F32)
    mixed_ref[...] = total[...].astype(BF16)

    several(spot_x.at[0:3], spot_sem.at[0]).wait_send()
    several(spot_x.at[0:3], spot_sem.at[2]).wait_send()
    several(count_in.at[0:7], cnt_sem.at[0]).wait_send()
    spare_copy(0).wait_send()
    spare_copy(1).wait_send()
    for way in range(2):
        several(ring_a.at[0:3], ring_send.at[way]).wait_send()
        several(ring_a.at[0:3], sum_send.at[way]).wait_send()
    for way in range(4):
        several(relay_a.at[:, 0:7], far_send.at[way]).wait_send()


def on_device(tokens, chosen_expert_index, routing_gate_weight, w_gate, w_up, w_down, capacity):
    rows, width = tokens.shape
    units = w_gate.shape[2]
    half = width // 2
    hbm = pl.BlockSpec(memory_space=pl.ANY)
    vmem = pl.BlockSpec(memory_space=pltpu.VMEM)
    smem = pl.BlockSpec(memory_space=pltpu.SMEM)
    dma = pltpu.SemaphoreType.DMA
    per_token = pltpu.VMEM((4, SPLIT, 8 * PIECE, rows), BF16)
    by_source = pltpu.VMEM((SPLIT, 2, 4, 4, PIECE, width), BF16)
    relay_a = pltpu.VMEM((SPLIT, 8, 4, PIECE, half), BF16)
    relay_b = pltpu.VMEM((SPLIT, 4, 2, 4, PIECE, half), BF16)
    return pl.pallas_call(
        kernel,
        out_shape=jax.ShapeDtypeStruct((rows, width), BF16),
        in_specs=[hbm, vmem, vmem, hbm, hbm, hbm, smem],
        out_specs=vmem,
        scratch_shapes=[
            pltpu.VMEM((rows, width), BF16),
            pltpu.VMEM((width, units), BF16),
            pltpu.VMEM((width, units), BF16),
            pltpu.VMEM((units, width), BF16),
            pltpu.VMEM((4, rows, half), BF16),
            pltpu.VMEM((4, rows, half), BF16),
            relay_a,
            relay_b,
            by_source,
            by_source,
            relay_a,
            relay_b,
            pltpu.VMEM((3, rows, half), BF16),
            pltpu.VMEM((3, rows, half), BF16),
            pltpu.VMEM((2, rows // 2, half), BF16),
            pltpu.VMEM((2, rows // 2, half), BF16),
            pltpu.VMEM((2, rows, half), BF16),
            pltpu.VMEM((2, rows, half), BF16),
            pltpu.VMEM((8, rows), F32),
            pltpu.VMEM((4, 8, rows), F32),
            pltpu.VMEM((4, 8, rows), F32),
            pltpu.VMEM((4, 8, rows), F32),
            pltpu.VMEM((4, 8, rows), F32),
            per_token,
            per_token,
            pltpu.VMEM((ROWS, units), BF16),
            pltpu.VMEM((rows, width), F32),
            pltpu.VMEM((8, 128), F32),
            pltpu.VMEM((8, 8, 128), F32),
            pltpu.VMEM((8, 128), F32),
            pltpu.VMEM((8, 128), F32),
            pltpu.VMEM((8, 128), F32),
            dma((4,)),
            dma((SPLIT, 4)),
            dma((4,)),
            dma((2,)),
            dma((4,)),
            dma((2,)),
            dma((2, 2, 3)),
            dma((2,)),
            dma((2, 2, 3)),
            dma((4,)),
            dma((2, SPLIT, 2)),
            dma((2, SPLIT + 2)),
        ],
        compiler_params=pltpu.CompilerParams(
            collective_id=0, has_side_effects=True, vmem_limit_bytes=60 * 2**20
        ),
        cost_estimate=pl.CostEstimate(
            flops=6 * EXPERTS * SLOT * width * units,
            bytes_accessed=6 * width * units,
            transcendentals=0,
        ),
    )(
        tokens,
        chosen_expert_index[:, :8].T,
        routing_gate_weight[:, :8].T,
        w_gate,
        w_up,
        w_down,
        capacity,
    )


def solution(mesh):
    return jax.shard_map(
        on_device,
        mesh=mesh,
        in_specs=(
            P(("dp", "expert"), None),
            P(("dp", "expert"), None),
            P(("dp", "expert"), None),
            P("expert", None, None),
            P("expert", None, None),
            P("expert", None, None),
            P("dp", "expert"),
        ),
        out_specs=P(("dp", "expert"), None),
        check_vma=False,
    )
```

```python
import jax
import jax.numpy as jnp
from jax import lax
from jax.experimental import pallas as pl
from jax.experimental.pallas import tpu as pltpu
from jax.sharding import PartitionSpec as P

BLOCK = 128
SLOT = 32
EXPERTS = 32
SPLIT = 2
PIECE = SLOT // SPLIT
ROWS = 16 * PIECE
MESH = pl.DeviceIdType.MESH
F32 = jnp.float32
BF16 = jnp.bfloat16


def iota(shape, axis):
    return lax.broadcasted_iota(jnp.int32, shape, axis)


def kernel(
    tokens_hbm, index_ref, gate_ref, w_gate_hbm, w_up_hbm, w_down_hbm, capacity_ref,
    mixed_ref,
    tok, w_gate, w_up, w_down, ring_a, ring_b, relay_a, relay_b, recv, answer, home_a, home_b,
    sum_a, sum_b, far_a, far_b, near_a, near_b,
    spot, spot_x, spot_y, spot_a, spot_b, scaled_a, scaled_b, hidden, total, count_relay, count_in, spare_out, spare_mid, spare_in,
    load_sem, local_sem, spot_sem, cnt_sem, spare_sem, ring_send, ring_recv, sum_send, sum_recv, far_send, far_recv, ret_recv,
):
    me = lax.axis_index("expert")
    group = lax.axis_index("dp")
    groups = lax.axis_size("dp")
    stride = groups // 4
    x, y, c = me // 8, (me // 2) % 4, me % 2
    half = tok.shape[1] // 2
    low, high = pl.ds(0, half), pl.ds(half, half)

    def remote(src, dst, sends, recvs, xd, yd, cd):
        return pltpu.make_async_remote_copy(
            src_ref=src,
            dst_ref=dst,
            send_sem=sends,
            recv_sem=recvs,
            device_id=(group, xd * 8 + yd * 2 + cd),
            device_id_type=MESH,
        )

    def several(ref, sem):
        return remote(ref, ref, sem, sem, x, y, 1 - c)

    first, second = pl.ds(0, tok.shape[0] // 2), pl.ds(tok.shape[0] // 2, tok.shape[0] // 2)

    def ring(way, order, axis):
        at, store, cols = [(x, ring_a, low), (y, ring_b, high)][axis]
        step = [1, 3][way]
        rows = [first, second] if way == 0 else [second, first]
        to = (at + step) % 4
        if order < 2:
            src, dst = tok.at[rows[order], cols], store.at[at, rows[order]]
        else:
            behind = (at + 4 - step) % 4
            src = dst = store.at[behind, rows[0]]
        return remote(
            src, dst, ring_send.at[axis], ring_recv.at[axis, way, order],
            to if axis == 0 else x, y if axis == 0 else to, c,
        )

    def spot_copy(d, axis):
        if axis == 0:
            return remote(spot, spot_x.at[x], spot_sem.at[0], spot_sem.at[1], (x + d) % 4, y, c)
        return remote(spot, spot_y.at[y], spot_sem.at[2], spot_sem.at[3], x, (y + d) % 4, c)

    def a2(q, d, dc, xs=slice(None)):
        yd, cd = (y + d) % 4, (c + dc) % 2
        return remote(
            relay_a.at[q, yd * 2 + cd, xs], recv.at[q, c, y, xs, :, low],
            far_send.at[0], far_recv.at[0, q, dc], x, yd, cd,
        )

    def b2(q, d, dc, ys=slice(None)):
        xd, cd = (x + d) % 4, (c + dc) % 2
        return remote(
            relay_b.at[q, xd, cd, ys], recv.at[q, c, ys, x, :, high],
            far_send.at[1], far_recv.at[1, q, dc], xd, y, cd,
        )

    def c1(q, d, dc, o=None):
        yd, cd = (y + d) % 4, (c + dc) % 2
        xs = slice(None) if o is None else (x + o) % 4
        return remote(
            answer.at[q, cd, yd, xs, :, low], home_a.at[q, y * 2 + c, xs],
            far_send.at[2], ret_recv.at[0, q if o is None else 2 if o == 2 else 3 if o == 0 else 1], x, yd, cd,
        )

    def d1(q, d, dc, o=None):
        xd, cd = (x + d) % 4, (c + dc) % 2
        ys = slice(None) if o is None else (y + o) % 4
        return remote(
            answer.at[q, cd, ys, xd, :, high], home_b.at[q, x, c, ys],
            far_send.at[3], ret_recv.at[1, q if o is None else 2 if o == 2 else 3 if o == 0 else 1], xd, y, cd,
        )

    def sums(way, order, axis):
        at = [x, y][axis]
        store, far, near = [(sum_a, far_a, near_a), (sum_b, far_b, near_b)][axis]
        rows = [first, second] if way == 0 else [second, first]
        to = (at + [1, 3][way]) % 4
        if order == 0:
            src, dst = store.at[0, rows[0]], far.at[way]
        else:
            half_of = rows[2 - order]
            src, dst = store.at[1 + way, half_of], near.at[way, half_of]
        return remote(
            src, dst, sum_send.at[axis], sum_recv.at[axis, way, order],
            to if axis == 0 else x, y if axis == 0 else to, c,
        )

    def own(q, hop):
        src, dst = [
            (relay_a.at[q, y * 2 + c], recv.at[q, c, y, :, :, low]),
            (relay_b.at[q, x, c], recv.at[q, c, :, x, :, high]),
            (answer.at[q, c, y, :, :, low], home_a.at[q, y * 2 + c]),
            (answer.at[q, c, :, x, :, high], home_b.at[q, x, c]),
        ][hop - 2]
        return pltpu.make_async_copy(src, dst, local_sem.at[q, hop - 2])

    def count_far(j):
        return remote(
            count_relay, count_in.at[c * 4 + y],
            cnt_sem.at[0], cnt_sem.at[1], x, (y + j // 2) % 4, (c + j % 2) % 2,
        )

    def spare_copy(hop):
        src, dst = [(spare_out, spare_mid), (spare_mid, spare_in)][hop]
        return pltpu.make_async_remote_copy(
            src_ref=src,
            dst_ref=dst,
            send_sem=spare_sem.at[hop],
            recv_sem=spare_sem.at[2 + hop],
            device_id=((group + stride) % groups, me),
            device_id_type=MESH,
        )

    loads = [
        pltpu.make_async_copy(src, dst, load_sem.at[i])
        for i, (src, dst) in enumerate(
            [
                (tokens_hbm, tok),
                (w_gate_hbm.at[0], w_gate),
                (w_up_hbm.at[0], w_up),
                (w_down_hbm.at[0], w_down),
            ]
        )
    ]
    for load in loads:
        load.start()

    barrier = pltpu.get_barrier_semaphore()

    @pl.loop(1, 8)
    def _(j):
        cd = (c + j % 2) % 2
        along_y = x * 8 + (y + j // 2) % 4 * 2 + cd
        pl.semaphore_signal(barrier, inc=1, device_id=(group, along_y), device_id_type=MESH)

        @pl.when(j > 1)
        def _():
            along_x = (x + j // 2) % 4 * 8 + y * 2 + cd
            pl.semaphore_signal(barrier, inc=1, device_id=(group, along_x), device_id_type=MESH)

    for to in (stride, groups - stride):
        pl.semaphore_signal(
            barrier, inc=1, device_id=((group + to) % groups, me), device_id_type=MESH
        )

    index = index_ref[...]
    spot[pl.ds(0, 2), :] = index[0:2, :].astype(F32)
    spot[pl.ds(2, 2), :] = gate_ref[0:2, :]
    spot[pl.ds(4, 4), :] = jnp.zeros((4, 256), F32)
    spot_x[x] = spot[...]
    spot_y[y] = spot[...]
    earlier = (iota((256, 256), 0) < iota((256, 256), 1)).astype(F32).astype(BF16)
    loads[0].wait()

    piece_id = iota((PIECE, 256), 0)
    pl.semaphore_wait(barrier, 15)

    @pl.loop(1, 4)
    def _(d):
        spot_copy(d, 0).start()
        spot_copy(d, 1).start()

    for order in range(2):
        for axis in range(2):
            for way in range(2):
                ring(way, order, axis).start()

    def pack(o):
        xs, ys = (x + o) % 4, (y + o) % 4
        rows_a = tok[:, low] if o == 0 else ring_a[xs]
        rows_b = tok[:, high] if o == 0 else ring_b[ys]
        lines_a, lines_b = spot_a[xs], spot_b[ys]
        lines_a = [lines_a[j : j + 1, :] for j in range(8)]
        lines_b = [lines_b[j : j + 1, :] for j in range(8)]
        for lines, rows, side in ((lines_a, rows_a, 0), (lines_b, rows_b, 1)):
            placer = jnp.concatenate(
                [
                    (line == (piece_id + q * PIECE).astype(F32)).astype(F32)
                    for q in range(SPLIT)
                    for line in lines
                ],
                axis=0,
            )
            packed = jnp.dot(placer.astype(BF16), rows, preferred_element_type=F32).astype(BF16)
            for q in range(SPLIT):
                part = packed[q * 8 * PIECE : (q + 1) * 8 * PIECE]
                if side == 0:
                    relay_a[q, :, xs] = part.reshape(8, PIECE, half)
                else:
                    relay_b[q, :, :, ys] = part.reshape(4, 2, PIECE, half)

    def start_second(q, o):
        @pl.loop(0, 2)
        def _(dc):
            @pl.loop(0, 4)
            def _(d):
                @pl.when(d + dc > 0)
                def _():
                    if o is None:
                        a2(q, d, dc).start()
                        b2(q, d, dc).start()
                    else:
                        a2(q, d, dc, (x + o) % 4).start()
                        b2(q, d, dc, (y + o) % 4).start()

    several(spot_x.at[0:3], spot_sem.at[1]).wait_recv()
    several(spot_y.at[0:3], spot_sem.at[3]).wait_recv()
    j = iota((8, 256), 0)
    for store, meta, ids in ((spot_a, spot_x, x * 8 + j), (spot_b, spot_y, j // 2 * 8 + y * 2 + j % 2)):
        ids = ids.astype(F32)
        named = jnp.concatenate(
            [
                ((meta[at, 0:1, :] == ids) | (meta[at, 1:2, :] == ids)).astype(F32)
                for at in range(4)
            ],
            axis=0,
        )
        place = jnp.dot(named.astype(BF16), earlier, preferred_element_type=F32)
        store[...] = jnp.where(named > 0.0, place, -1.0).reshape(4, 8, 256)
    lane = iota((8, 128), 1)
    numbers = jnp.zeros((8, 128), F32)
    for xs in range(4):
        number = jnp.sum((spot_a[xs] >= 0.0).astype(F32), axis=1, keepdims=True)
        numbers = jnp.where(lane == xs, number, numbers)
    count_relay[...] = numbers

    @pl.loop(1, 8)
    def _(j):
        count_far(j).start()

    count_in[c * 4 + y] = count_relay[...]
    pack(0)
    for axis in range(2):
        for way in range(2):
            ring(way, 0, axis).wait_recv()
            ring(way, 2, axis).start()

    start_second(0, 0)

    @pl.loop(0, 4)
    def _(at):
        lines_a, lines_b = spot_a[at], spot_b[at]
        weight_a = spot_x[at, pl.ds(2 + x // 2, 1), :]
        for j in range(8):
            line_b = lines_b[j : j + 1, :]
            weight_b = spot_y[at, pl.ds(2 + j // 4, 1), :]
            for q in range(SPLIT):
                slot_id = (piece_id + q * PIECE).astype(F32)
                rows = pl.ds(j * PIECE, PIECE)
                spread = jnp.where(lines_a[j : j + 1, :] == slot_id, weight_a, 0.0)
                scaled_a[at, q, rows, :] = spread.astype(BF16)
                spread = jnp.where(line_b == slot_id, weight_b, 0.0)
                scaled_b[at, q, rows, :] = spread.astype(BF16)

    several(count_in.at[0:7], cnt_sem.at[1]).wait_recv()

    def place_of(r):
        return r % 4 * 8 + r // 4 % 4 * 2 + r // 16

    arrived = count_in[...].reshape(2 * EXPERTS, 128).astype(BF16)
    row, col = iota((EXPERTS, 2 * EXPERTS), 0), iota((EXPERTS, 2 * EXPERTS), 1)
    pick = (col == row // 4 * 8 + y * 2 + c).astype(F32).astype(BF16)
    by_lane = jnp.dot(pick, arrived, preferred_element_type=F32)
    chosen = iota((EXPERTS, 128), 1) == iota((EXPERTS, 128), 0) % 4
    count = jnp.sum(jnp.where(chosen, by_lane, 0.0), axis=1, keepdims=True)
    count = jnp.broadcast_to(count, (EXPERTS, 128))
    row, col = iota((EXPERTS, EXPERTS), 0), iota((EXPERTS, EXPERTS), 1)
    before = (place_of(col) < place_of(row)).astype(F32).astype(BF16)
    offset = jnp.dot(before, count.astype(BF16), preferred_element_type=F32)
    limit = capacity_ref[0, 0].astype(F32)
    spare = jnp.maximum(limit - jnp.sum(count, axis=0, keepdims=True), 0.0)
    spare_out[...] = jnp.broadcast_to(spare, (8, 128))
    spare_copy(0).start()
    for axis in range(2):
        ring(0, 1, axis).wait_recv()
    pack(3)
    start_second(0, 3)
    for axis in range(2):
        ring(1, 1, axis).wait_recv()
    pack(1)
    start_second(0, 1)
    spare_copy(0).wait_recv()
    spare_copy(1).start()
    for axis in range(2):
        for way in range(2):
            ring(way, 2, axis).wait_recv()
    start_second(1, 0)
    pack(2)
    start_second(0, 2)
    for o in (3, 1, 2):
        start_second(1, o)
    for q in range(SPLIT):
        own(q, 2).start()
        own(q, 3).start()

    spare_copy(1).wait_recv()
    room = limit + jnp.minimum(spare_in[0:1, :], float(BLOCK))
    kept = jnp.minimum(jnp.maximum(room - offset, 0.0), count).astype(BF16)
    for load in loads[1:]:
        load.wait()

    for q in range(SPLIT):
        own(q, 2).wait()
        own(q, 3).wait()

        @pl.loop(0, 2)
        def _(dc):
            core = (c + dc) % 2

            @pl.when(dc == 0)
            def _():
                several(relay_a.at[q, 0:3], far_recv.at[0, q, 0]).wait_recv()
                several(relay_a.at[q, 0:3], far_recv.at[1, q, 0]).wait_recv()

            @pl.when(dc == 1)
            def _():
                several(relay_a.at[q, 0:4], far_recv.at[0, q, 1]).wait_recv()
                several(relay_a.at[q, 0:4], far_recv.at[1, q, 1]).wait_recv()

            source = core * 16 + iota((ROWS, EXPERTS), 0) // PIECE
            pick = (source == iota((ROWS, EXPERTS), 1)).astype(F32).astype(BF16)
            most = jnp.dot(pick, kept, preferred_element_type=F32)[:, 0:1]
            keep = (iota((ROWS, 1), 0) % PIECE + q * PIECE).astype(F32) < most
            rows = recv[q, core].reshape(ROWS, 2 * half)
            for f in range(3):
                cols = pl.ds(f * 256, 256)
                gated = jnp.dot(rows, w_gate[:, cols], preferred_element_type=F32)
                upward = jnp.dot(rows, w_up[:, cols], preferred_element_type=F32)
                value = gated / (1.0 + jnp.exp(-gated)) * upward
                hidden[:, cols] = jnp.where(keep, value, 0.0).astype(BF16)
            h = hidden[...]
            for d in range(4):
                cols = pl.ds(d * 512, 512)
                result = jnp.dot(h, w_down[:, cols], preferred_element_type=F32)
                answer[q, core, :, :, :, cols] = result.astype(BF16).reshape(4, 4, PIECE, 512)

            for o in (None,) if q == 0 else (2,):

                @pl.loop(0, 4)
                def _(d):
                    @pl.when(d + dc > 0)
                    def _():
                        c1(q, d, dc, o).start()
                        d1(q, d, dc, o).start()

        if q == SPLIT - 1:
            for o in (1, 3, 0):

                @pl.loop(1, 8)
                def _(j):
                    c1(q, j // 2, j % 2, o).start()
                    d1(q, j // 2, j % 2, o).start()

        own(q, 4).start()
        own(q, 5).start()

    for q in range(SPLIT):
        own(q, 4).wait()
        own(q, 5).wait()
    for axis in range(2):
        several(relay_a.at[0, 0:7], ret_recv.at[axis, 0]).wait_recv()
        several(relay_a.at[0, 0:7, 0], ret_recv.at[axis, 2]).wait_recv()

    def sum_for(o, axis):
        at = ([x, y][axis] + o) % 4
        result = None
        for q in range(SPLIT):
            rows = home_a[q, :, at] if axis == 0 else home_b[q, :, :, at]
            share = lax.dot_general(
                (scaled_a if axis == 0 else scaled_b)[at, q],
                rows.reshape(8 * PIECE, half),
                (((0,), (0,)), ((), ())),
                preferred_element_type=F32,
            )
            result = share if result is None else result + share
        return result

    for axis in range(2):
        store = [sum_a, sum_b][axis]
        store[0] = sum_for(2, axis).astype(BF16)
        for way in range(2):
            sums(way, 0, axis).start()
    for axis in range(2):
        several(relay_a.at[0, 0:7, 0:2], ret_recv.at[axis, 1]).wait_recv()
    for way in range(2):
        for axis in range(2):
            store = [sum_a, sum_b][axis]
            store[1 + way] = sum_for([1, 3][way], axis).astype(BF16)
            sums(way, 1, axis).start()
    for axis in range(2):
        several(relay_a.at[0, 0:7, 0], ret_recv.at[axis, 3]).wait_recv()
        total[:, [low, high][axis]] = sum_for(0, axis)
    for way in range(2):
        for axis in range(2):
            store, far = [(sum_a, far_a), (sum_b, far_b)][axis]
            rows = [first, second][way]
            sums(way, 0, axis).wait_recv()
            merged = store[1 + way, rows, :].astype(F32) + far[way].astype(F32)
            store[1 + way, rows, :] = merged.astype(BF16)
            sums(way, 2, axis).start()
    for order in (1, 2):
        for axis in range(2):
            near, cols = [(near_a, low), (near_b, high)][axis]
            for way in range(2):
                sums(way, order, axis).wait_recv()
                rows = [first, second][way if order == 2 else 1 - way]
                total[rows, cols] += near[way, rows, :].astype(F32)
    mixed_ref[...] = total[...].astype(BF16)

    several(spot_x.at[0:3], spot_sem.at[0]).wait_send()
    several(spot_x.at[0:3], spot_sem.at[2]).wait_send()
    several(count_in.at[0:7], cnt_sem.at[0]).wait_send()
    spare_copy(0).wait_send()
    spare_copy(1).wait_send()
    for way in range(2):
        several(ring_a.at[0:3], ring_send.at[way]).wait_send()
        several(ring_a.at[0:3], sum_send.at[way]).wait_send()
    for way in range(4):
        several(relay_a.at[:, 0:7], far_send.at[way]).wait_send()


def on_device(tokens, chosen_expert_index, routing_gate_weight, w_gate, w_up, w_down, capacity):
    rows, width = tokens.shape
    units = w_gate.shape[2]
    half = width // 2
    hbm = pl.BlockSpec(memory_space=pl.ANY)
    vmem = pl.BlockSpec(memory_space=pltpu.VMEM)
    smem = pl.BlockSpec(memory_space=pltpu.SMEM)
    dma = pltpu.SemaphoreType.DMA
    per_token = pltpu.VMEM((4, SPLIT, 8 * PIECE, rows), BF16)
    by_source = pltpu.VMEM((SPLIT, 2, 4, 4, PIECE, width), BF16)
    relay_a = pltpu.VMEM((SPLIT, 8, 4, PIECE, half), BF16)
    relay_b = pltpu.VMEM((SPLIT, 4, 2, 4, PIECE, half), BF16)
    return pl.pallas_call(
        kernel,
        out_shape=jax.ShapeDtypeStruct((rows, width), BF16),
        in_specs=[hbm, vmem, vmem, hbm, hbm, hbm, smem],
        out_specs=vmem,
        scratch_shapes=[
            pltpu.VMEM((rows, width), BF16),
            pltpu.VMEM((width, units), BF16),
            pltpu.VMEM((width, units), BF16),
            pltpu.VMEM((units, width), BF16),
            pltpu.VMEM((4, rows, half), BF16),
            pltpu.VMEM((4, rows, half), BF16),
            relay_a,
            relay_b,
            by_source,
            by_source,
            relay_a,
            relay_b,
            pltpu.VMEM((3, rows, half), BF16),
            pltpu.VMEM((3, rows, half), BF16),
            pltpu.VMEM((2, rows // 2, half), BF16),
            pltpu.VMEM((2, rows // 2, half), BF16),
            pltpu.VMEM((2, rows, half), BF16),
            pltpu.VMEM((2, rows, half), BF16),
            pltpu.VMEM((8, rows), F32),
            pltpu.VMEM((4, 8, rows), F32),
            pltpu.VMEM((4, 8, rows), F32),
            pltpu.VMEM((4, 8, rows), F32),
            pltpu.VMEM((4, 8, rows), F32),
            per_token,
            per_token,
            pltpu.VMEM((ROWS, units), BF16),
            pltpu.VMEM((rows, width), F32),
            pltpu.VMEM((8, 128), F32),
            pltpu.VMEM((8, 8, 128), F32),
            pltpu.VMEM((8, 128), F32),
            pltpu.VMEM((8, 128), F32),
            pltpu.VMEM((8, 128), F32),
            dma((4,)),
            dma((SPLIT, 4)),
            dma((4,)),
            dma((2,)),
            dma((4,)),
            dma((2,)),
            dma((2, 2, 3)),
            dma((2,)),
            dma((2, 2, 3)),
            dma((4,)),
            dma((2, SPLIT, 2)),
            dma((2, SPLIT + 2)),
        ],
        compiler_params=pltpu.CompilerParams(
            collective_id=0, has_side_effects=True, vmem_limit_bytes=60 * 2**20
        ),
        cost_estimate=pl.CostEstimate(
            flops=6 * EXPERTS * SLOT * width * units,
            bytes_accessed=6 * width * units,
            transcendentals=0,
        ),
    )(
        tokens,
        chosen_expert_index[:, :8].T,
        routing_gate_weight[:, :8].T,
        w_gate,
        w_up,
        w_down,
        capacity,
    )


def solution(mesh):
    return jax.shard_map(
        on_device,
        mesh=mesh,
        in_specs=(
            P(("dp", "expert"), None),
            P(("dp", "expert"), None),
            P(("dp", "expert"), None),
            P("expert", None, None),
            P("expert", None, None),
            P("expert", None, None),
            P("dp", "expert"),
        ),
        out_specs=P(("dp", "expert"), None),
        check_vma=False,
    )
```
